32 devices in a mesh: seq: 4 (over z), head: 4 (over y, x), dp: 2 (over core).
Axes of the slice: x: 2, y: 2, z: 4, core: 2. Of those that a mesh axis runs over, the one named last changes fastest.
Arguments:
- queries: bfloat16 [2, 512, 4096], P('dp', 'seq', 'head'), may hold values from -0.23925781 to 0.23925781
- key_rows: bfloat16 [2, 512, 4096], P('dp', 'seq', 'head'), may hold values from -0.23925781 to 0.23925781
- values: bfloat16 [2, 512, 4096], P('dp', 'seq', 'head'), may hold values from -6 to 6
- out_grad: bfloat16 [2, 512, 4096], P('dp', 'seq', 'head'), may hold values from -6 to 6
- decay_rate: float32 [32], P('head'), may hold values from 4e-05 to 0.025, as said below
- rotation: float32 [4, 4096], P(None, 'head')
- refusal: float32 [4096, 2], P('head')
- proj_weight: float32 [4, 4096], P(None, 'head'), may hold values from -0.09375 to 0.09375
- proj_bias: float32 [4], replicated, may hold values from -4 to 4
- positions: int32 [2, 16], P('dp'), may hold values from 0 to 511, as said below
Outputs:
- attended: bfloat16 [2, 512, 4096], P('dp', 'seq', 'head')
- grad_query: bfloat16 [2, 512, 4096], P('dp', 'seq', 'head')
- grad_key: bfloat16 [2, 512, 4096], P('dp', 'seq', 'head')
- grad_value: bfloat16 [2, 512, 4096], P('dp', 'seq', 'head')
- grad_rotation: float32 [4, 4096], P(None, 'head')
- grad_weight: float32 [4, 4096], P(None, 'head')
- grad_bias: float32 [4], replicated
The draws below stay inside these ranges and needn't reach their ends.
Inputs may be any that keep to these rules, and one draw needn't show every extreme that they name: 16 distinct positions in ascending order; among them always 0, 256 and 511. `decay_rate`: one rate per head, the same at every position.
All inputs are finite; a program needn't handle non-finite values.
Results may differ from the reference program's by a relative error of at most 0.0032.
Values sent between devices are 32-bit elements; how exact they have to be, the bound alone decides.
A program may use at most 128 MiB of HBM per device.

```python
import math
import jax
import jax.numpy as jnp
from jax import lax

HEADS = 32
HDIM = 128
RANK = 4
REFUSE = 2
NPOS = 16
GROUP = 128
DOCS = 2
LENGTH = 512
WIDTH = 4096


def shared_maps(key):
    first, second, third = jax.random.split(jax.random.fold_in(key, 17), 3)
    rotation = jax.random.normal(first, (RANK, WIDTH), jnp.float32) / math.sqrt(WIDTH)
    mixing = jax.random.normal(second, (RANK, REFUSE), jnp.float32) / math.sqrt(RANK)
    noise = jax.random.normal(third, (WIDTH, REFUSE), jnp.float32) / math.sqrt(WIDTH)
    blended = jnp.sum(rotation.T[:, :, None] * mixing[None, :, :], axis=1)
    return (rotation, 0.8 * blended + 0.6 * noise)


def draw_rotation(key, part):
    return shared_maps(key)[0]


def draw_refusal(key, part):
    return shared_maps(key)[1]


def draw_decay_rate(key, part):
    uniform_draw = jax.random.uniform(jax.random.fold_in(key, 3), (HEADS,), jnp.float32)
    lowest, highest_rate = (math.log(0.0001), math.log(0.025))
    return jnp.exp(lowest + uniform_draw * (highest_rate - lowest))


def draw_positions(key, part):
    half = LENGTH // 2

    def one_document(document_key):
        middle = jax.random.permutation(document_key, LENGTH - 3)[:NPOS - 3].astype(jnp.int32) + 1
        middle = jnp.where(middle >= half, middle + 1, middle)
        fixed = jnp.array([0, half, LENGTH - 1], jnp.int32)
        return jnp.sort(jnp.concatenate([fixed, middle]))
    document_keys = jax.random.split(jax.random.fold_in(key, 5), DOCS)
    return jax.vmap(one_document)(document_keys)


def shard_levels(rng, extent, cuts, smallest, top_value):
    gain, own = 1.0, jax.random.fold_in(rng, 6)
    for axis_at, shards_of in cuts:
        draws = jnp.exp(jax.random.uniform(jax.random.fold_in(own, axis_at), (shards_of,), jnp.float32, smallest / len(cuts), top_value / len(cuts)))
        gain = gain * jnp.repeat(draws, extent[axis_at] // shards_of).reshape([-1 if axis == axis_at else 1 for axis in range(len(extent))])
    return gain


def gaussian(rng, extent, deviation, most, cuts=(), dtype=jnp.bfloat16):
    values = jax.random.normal(rng, extent, jnp.float32) * deviation
    if len(cuts) > 0:
        values = shard_levels(rng, extent, cuts, -0.22, 0.18) * values
    return jnp.clip(values, min=-most, max=most).astype(dtype)


def setup_inputs(seed: int = 0) -> dict:
    keys = jax.random.split(jax.random.key(seed), 11)
    queries = gaussian(keys[0], (DOCS, LENGTH, WIDTH), 0.04, 0.23925781, ((0, 2), (1, 4), (2, 4)))
    key_rows = gaussian(keys[1], (DOCS, LENGTH, WIDTH), 0.04, 0.23925781, ((0, 2), (1, 4), (2, 4)))
    values = gaussian(keys[2], (DOCS, LENGTH, WIDTH), 1.0, 6.0, ((0, 2), (1, 4), (2, 4)))
    out_grad = gaussian(keys[3], (DOCS, LENGTH, WIDTH), 1.0, 6.0, ((0, 2), (1, 4), (2, 4)))
    decay_rate = draw_decay_rate(jax.random.fold_in(keys[10], 71), 0)
    rotation = draw_rotation(jax.random.fold_in(keys[10], 71), 0)
    refusal = draw_refusal(jax.random.fold_in(keys[10], 71), 0)
    proj_weight = gaussian(keys[7], (RANK, WIDTH), WIDTH ** -0.5, 0.09375, ((1, 4),), jnp.float32)
    proj_bias = gaussian(keys[8], (RANK,), 1.0, 4.0, (), jnp.float32)
    positions = draw_positions(jax.random.fold_in(keys[10], 71), 0)
    return {"queries": queries, "key_rows": key_rows, "values": values, "out_grad": out_grad, "decay_rate": decay_rate, "rotation": rotation, "refusal": refusal, "proj_weight": proj_weight, "proj_bias": proj_bias, "positions": positions}


highest = lax.Precision.HIGHEST


def decay_table(log_decay, count):
    offsets = jnp.arange(count)
    between = offsets[:, None] - offsets[None, :]
    powers = jnp.exp(jnp.maximum(between, 0).astype(jnp.float32)[None] * log_decay[:, None, None])
    return jnp.where(between[None] >= 0, powers, 0.0)


def gram_inverse(gram):
    determinant = gram[0, 0] * gram[1, 1] - gram[0, 1] * gram[1, 0]
    adjugate = jnp.stack([jnp.stack([gram[1, 1], -gram[0, 1]]), jnp.stack([-gram[1, 0], gram[0, 0]])])
    return adjugate / determinant


def reference(queries, key_rows, values, out_grad, decay_rate, rotation, refusal, proj_weight, proj_bias, positions):
    gram = jnp.dot(refusal.T, refusal, precision=highest)
    coupling = jnp.dot(rotation, refusal, precision=highest)
    inverse = gram_inverse(gram)
    rotated = rotation - jnp.dot(jnp.dot(coupling, inverse, precision=highest), refusal.T, precision=highest)
    log_decay = jnp.log1p(-decay_rate)
    table = decay_table(log_decay, GROUP)
    offsets = jnp.arange(GROUP).astype(jnp.float32)
    enter = jnp.exp((offsets + 1.0)[:, None] * log_decay[None, :])
    leave = jnp.exp((GROUP - offsets)[:, None] * log_decay[None, :])
    start_weight = jnp.exp(offsets[:, None] * log_decay[None, :])
    end_weight = jnp.exp((GROUP - 1.0 - offsets)[:, None] * log_decay[None, :])
    keep = jnp.exp(GROUP * log_decay)
    blocks = LENGTH // GROUP
    attended_all, grad_q_all, grad_k_all, grad_v_all = [], [], [], []
    grad_weight = jnp.zeros((RANK, WIDTH), jnp.float32)
    grad_bias = jnp.zeros((RANK,), jnp.float32)
    grad_rotated = jnp.zeros((RANK, WIDTH), jnp.float32)
    for document in range(DOCS):
        places = positions[document]
        picked = values[document][places].astype(jnp.float32)
        code = jnp.dot(picked, proj_weight.T, precision=highest) + proj_bias - jnp.dot(picked, rotated.T, precision=highest)
        shift_rows = jnp.dot(code, rotated, precision=highest)
        moved = values[document].at[places].set((picked + shift_rows).astype(jnp.bfloat16))
        query_blocks = queries[document].reshape(blocks, GROUP, HEADS, HDIM)
        key_blocks = key_rows[document].reshape(blocks, GROUP, HEADS, HDIM)
        moved_blocks = moved.reshape(blocks, GROUP, HEADS, HDIM)
        grad_blocks = out_grad[document].reshape(blocks, GROUP, HEADS, HDIM)

        def forward_block(state, block):
            query_b, key_b, moved_b = block
            scores = jnp.einsum('thd,shd->hts', query_b.astype(jnp.float32), key_b.astype(jnp.float32))
            mixing = (scores * table).astype(jnp.bfloat16)
            inner = jnp.einsum('hts,she->the', mixing.astype(jnp.float32), moved_b.astype(jnp.float32))
            outer = enter[:, :, None] * jnp.einsum('thd,hde->the', query_b.astype(jnp.float32), state, precision=highest)
            local = jnp.einsum('shd,she->hde', key_b.astype(jnp.float32) * end_weight[:, :, None], moved_b.astype(jnp.float32), precision=highest)
            return keep[:, None, None] * state + local, ((inner + outer).astype(jnp.bfloat16), state)

        start_state = jnp.zeros((HEADS, HDIM, HDIM), jnp.float32)
        _, (attended_blocks, entering) = lax.scan(forward_block, start_state, (query_blocks, key_blocks, moved_blocks))

        def backward_block(later, block):
            query_b, key_b, moved_b, grad_b, state = block
            scores = jnp.einsum('thd,shd->hts', query_b.astype(jnp.float32), key_b.astype(jnp.float32))
            mixing = (scores * table).astype(jnp.bfloat16)
            grad_scores = jnp.einsum('the,she->hts', grad_b.astype(jnp.float32), moved_b.astype(jnp.float32))
            grad_mixing = (grad_scores * table).astype(jnp.bfloat16)
            grad_q = jnp.einsum('hts,shd->thd', grad_mixing.astype(jnp.float32), key_b.astype(jnp.float32))
            grad_q = grad_q + enter[:, :, None] * jnp.einsum('the,hde->thd', grad_b.astype(jnp.float32), state, precision=highest)
            grad_k = jnp.einsum('hts,thd->shd', grad_mixing.astype(jnp.float32), query_b.astype(jnp.float32))
            grad_k = grad_k + leave[:, :, None] * jnp.einsum('she,hde->shd', moved_b.astype(jnp.float32), later, precision=highest)
            grad_m = jnp.einsum('hts,the->she', mixing.astype(jnp.float32), grad_b.astype(jnp.float32))
            grad_m = grad_m + leave[:, :, None] * jnp.einsum('shd,hde->she', key_b.astype(jnp.float32), later, precision=highest)
            local = jnp.einsum('thd,the->hde', query_b.astype(jnp.float32) * start_weight[:, :, None], grad_b.astype(jnp.float32), precision=highest)
            return keep[:, None, None] * later + local, (grad_q.astype(jnp.bfloat16), grad_k.astype(jnp.bfloat16), grad_m)

        _, (grad_q_blocks, grad_k_blocks, grad_m_blocks) = lax.scan(backward_block, start_state, (query_blocks, key_blocks, moved_blocks, grad_blocks, entering), reverse=True)
        grad_moved = grad_m_blocks.reshape(LENGTH, WIDTH)
        picked_grad = grad_moved[places]
        code_grad = jnp.dot(picked_grad, rotated.T, precision=highest)
        grad_weight = grad_weight + jnp.dot(code_grad.T, picked, precision=highest)
        grad_bias = grad_bias + jnp.sum(code_grad, axis=0)
        grad_rotated = grad_rotated + jnp.dot(code.T, picked_grad, precision=highest) - jnp.dot(code_grad.T, picked, precision=highest)
        grad_value = grad_moved.at[places].add(jnp.dot(code_grad, proj_weight - rotated, precision=highest))
        attended_all.append(attended_blocks.reshape(LENGTH, WIDTH))
        grad_q_all.append(grad_q_blocks.reshape(LENGTH, WIDTH))
        grad_k_all.append(grad_k_blocks.reshape(LENGTH, WIDTH))
        grad_v_all.append(grad_value.astype(jnp.bfloat16))
    along = jnp.dot(grad_rotated, refusal, precision=highest)
    grad_rotation = grad_rotated - jnp.dot(jnp.dot(along, inverse, precision=highest), refusal.T, precision=highest)
    return (jnp.stack(attended_all), jnp.stack(grad_q_all), jnp.stack(grad_k_all), jnp.stack(grad_v_all), grad_rotation, grad_weight, grad_bias)
```

```python
import functools
import jax
import jax.numpy as jnp
from jax import lax
from jax.experimental import pallas as pl
from jax.experimental.pallas import tpu as pltpu
from jax.sharding import PartitionSpec as P

highest = lax.Precision.HIGHEST
MESH = pl.DeviceIdType.MESH
f32 = jnp.float32
bf16 = jnp.bfloat16


def contract(a, b, da, db, precision=None):
    return lax.dot_general(
        a, b, (((da,), (db,)), ((), ())), precision=precision, preferred_element_type=f32
    )


def split(x):
    high = x.astype(bf16)
    return high, (x - high.astype(f32)).astype(bf16)


def halves(x):
    n = x.shape[1] // 2
    return x[:, :n] + x[:, n:]


def kernel(
    sizes,
    q_ref,
    k_ref,
    v_ref,
    g_ref,
    decay_ref,
    rotation_ref,
    refusal_ref,
    weight_ref,
    bias_ref,
    positions_ref,
    attended_ref,
    grad_query_ref,
    grad_key_ref,
    grad_value_ref,
    grad_rotation_ref,
    grad_weight_ref,
    grad_bias_ref,
    stack,
    picks,
    rows,
    moved,
    table,
    mixing,
    grad_mixing,
    grad_moved,
    state,
    state_in,
    later,
    later_in,
    first,
    second,
    pay,
    parts,
    total,
    first_send,
    first_recv,
    second_send,
    second_recv,
    state_send,
    state_recv,
    later_send,
    later_recv,
    parts_send,
    parts_recv,
    total_send,
    total_recv,
):
    seqs, peers, docs, heads, owners = sizes
    group = q_ref.shape[1]
    size = q_ref.shape[2] // heads
    npos = positions_ref.shape[1]
    members = seqs * docs
    stride = members // owners
    z, y, c = lax.axis_index("seq"), lax.axis_index("head"), lax.axis_index("dp")
    last = seqs - 1
    member = z * docs + c

    barrier = pltpu.get_barrier_semaphore()
    for step in range(1, peers):
        pl.semaphore_signal(
            barrier, inc=1, device_id={"head": lax.rem(y + step, peers)}, device_id_type=MESH
        )

    def greet(step, carry):
        other = lax.rem(member + step, members)
        pl.semaphore_signal(
            barrier,
            inc=1,
            device_id={"seq": other // docs, "dp": lax.rem(other, docs)},
            device_id_type=MESH,
        )
        return carry

    lax.fori_loop(1, members, greet, 0)

    places = z * group + lax.broadcasted_iota(jnp.int32, (group, npos), 0)
    chosen = places == positions_ref[...]
    select = jnp.where(chosen, 1.0, 0.0)
    stack[npos:, :] = jnp.zeros((stack.shape[0] - npos, stack.shape[1]), f32)
    picked = contract(select.astype(bf16), v_ref[0], 0, 0)
    stack[:npos, :] = picked
    stack[npos : npos + 4, :] = weight_ref[...]
    stack[npos + 4 : npos + 8, :] = rotation_ref[...]
    stack[npos + 8 : npos + 10, :] = refusal_ref[...]
    first[y] = jnp.zeros(first.shape[1:], f32)
    first[y, :, : stack.shape[0]] = contract(stack[npos:, :], stack[...], 1, 1, highest)
    pl.semaphore_wait(barrier, peers - 1 + members - 1)

    def across(buffer, send, recv, step):
        other = lax.rem(y + step, peers)
        return pltpu.make_async_remote_copy(
            src_ref=buffer.at[y],
            dst_ref=buffer.at[y],
            send_sem=send.at[step - 1],
            recv_sem=recv.at[y],
            device_id={"head": other},
            device_id_type=MESH,
        )

    def arrived(buffer, send, recv, step):
        other = lax.rem(y + step, peers)
        pltpu.make_async_remote_copy(
            src_ref=buffer.at[other],
            dst_ref=buffer.at[other],
            send_sem=send.at[step - 1],
            recv_sem=recv.at[other],
            device_id={"head": other},
            device_id_type=MESH,
        ).wait_recv()

    for step in range(1, peers):
        across(first, first_send, first_recv, step).start()

    def state_copy(h):
        return pltpu.make_async_remote_copy(
            src_ref=state.at[h],
            dst_ref=state_in.at[h],
            send_sem=state_send.at[h],
            recv_sem=state_recv.at[h],
            device_id={"seq": lax.rem(z + 1, seqs)},
            device_id_type=MESH,
        )

    def later_copy(h):
        return pltpu.make_async_remote_copy(
            src_ref=later.at[h],
            dst_ref=later_in.at[h],
            send_sem=later_send.at[h],
            recv_sem=later_recv.at[h],
            device_id={"seq": lax.rem(z + seqs - 1, seqs)},
            device_id_type=MESH,
        )

    offsets = lax.broadcasted_iota(jnp.int32, (group, size), 0).astype(f32)

    def log_decay(h):
        return jnp.log1p(-jnp.full((1, size), decay_ref[h], f32))

    for h in range(heads):
        at = slice(h * size, (h + 1) * size)
        weighted = g_ref[0, :, at].astype(f32) * jnp.exp(offsets * log_decay(h))
        both = jnp.concatenate(split(weighted), axis=1)
        later[h] = halves(contract(q_ref[0, :, at], both, 0, 0))

        @pl.when(z == last)
        def _():
            later_copy(h).start()

    @pl.when(z == last)
    def _():
        later_in[...] = jnp.zeros_like(later_in)

    @pl.when(z == 0)
    def _():
        state_in[...] = jnp.zeros_like(state_in)

    columns = lax.broadcasted_iota(jnp.int32, (group, group), 1)
    between = lax.broadcasted_iota(jnp.int32, (group, group), 0) - columns
    apart = jnp.maximum(between, 0).astype(f32)
    for h in range(heads):
        at = slice(h * size, (h + 1) * size)
        powers = jnp.where(between >= 0, jnp.exp(apart * log_decay(h)), 0.0)
        table[h] = powers
        mixing[h] = (contract(q_ref[0, :, at], k_ref[0, :, at], 1, 1) * powers).astype(bf16)

    for step in range(1, peers):
        arrived(first, first_send, first_recv, step)
    summed = first[0]
    for peer in range(1, peers):
        summed = summed + first[peer]
    at_ref = npos + 8
    gram = [
        [summed[8 + a : 9 + a, at_ref + b : at_ref + b + 1] for b in range(2)] for a in range(2)
    ]
    determinant = gram[0][0] * gram[1][1] - gram[0][1] * gram[1][0]
    inverse = [
        [gram[1][1] / determinant, -gram[0][1] / determinant],
        [-gram[1][0] / determinant, gram[0][0] / determinant],
    ]
    coupling = [summed[4:8, at_ref + b : at_ref + b + 1] for b in range(2)]
    map_0 = coupling[0] * inverse[0][0] + coupling[1] * inverse[1][0]
    map_1 = coupling[0] * inverse[0][1] + coupling[1] * inverse[1][1]
    rotated = rotation_ref[...] - map_0 * refusal_ref[0:1, :] - map_1 * refusal_ref[1:2, :]
    rows[...] = jnp.zeros_like(rows)
    rows[0:4, :] = rotated
    rows[4:6, :] = refusal_ref[...]
    along = summed[8:10, :npos]
    rank = lax.broadcasted_iota(jnp.int32, (4, npos), 0)
    bias = jnp.zeros((4, npos), f32)
    for r in range(4):
        bias = jnp.where(rank == r, bias_ref[r], bias)
    code = (
        summed[0:4, :npos]
        + bias
        - (summed[4:8, :npos] - map_0 * along[0:1, :] - map_1 * along[1:2, :])
    )
    spread = contract(select, code, 1, 1, highest)
    for h in range(heads):
        at = slice(h * size, (h + 1) * size)
        value = v_ref[0, :, at].astype(f32)
        shift = spread[:, 0:1] * rows[0:1, at]
        for r in range(1, 4):
            shift = shift + spread[:, r : r + 1] * rows[r : r + 1, at]
        value = (value + shift).astype(bf16)
        moved[:, at] = value
        weighted = value.astype(f32) * jnp.exp((group - 1.0 - offsets) * log_decay(h))
        both = jnp.concatenate(split(weighted), axis=1)
        state[h] = halves(contract(k_ref[0, :, at], both, 0, 0))

        @pl.when(z == 0)
        def _():
            state_copy(h).start()

    def later_step(h):
        at = pl.ds(pl.multiple_of(h * size, size), size)
        decay = log_decay(h)

        @pl.when(z < last)
        def _():
            later_copy(h).wait_recv()

        @pl.when(jnp.logical_and(z > 0, z < last))
        def _():
            later[h] = later[h] + jnp.exp(group * decay) * later_in[h]
            later_copy(h).start()

        high, low = split(later_in[h])
        leave = jnp.exp((group - offsets) * decay)
        grad = g_ref[0, :, at]
        value = moved[:, at]
        wide = contract(mixing[h], grad, 0, 0) + leave * halves(
            contract(k_ref[0, :, at], jnp.concatenate([high, low], axis=1), 1, 0)
        )
        grad_moved[:, at] = wide
        picks[:npos, at] = contract(select, wide, 0, 0, highest)
        mixed = (contract(grad, value, 1, 1) * table[h]).astype(bf16)
        grad_mixing[h] = mixed
        grad_key = contract(mixed, q_ref[0, :, at], 0, 0) + leave * halves(
            contract(value, jnp.concatenate([high, low], axis=0), 1, 1)
        )
        grad_key_ref[0, :, at] = grad_key.astype(bf16)

    def state_step(h):
        at = pl.ds(pl.multiple_of(h * size, size), size)
        decay = log_decay(h)

        @pl.when(z > 0)
        def _():
            state_copy(h).wait_recv()

        @pl.when(jnp.logical_and(z > 0, z < last))
        def _():
            state[h] = state[h] + jnp.exp(group * decay) * state_in[h]
            state_copy(h).start()

        high, low = split(state_in[h])
        enter = jnp.exp((offsets + 1.0) * decay)
        attended = contract(mixing[h], moved[:, at], 1, 0) + enter * halves(
            contract(q_ref[0, :, at], jnp.concatenate([high, low], axis=1), 1, 0)
        )
        attended_ref[0, :, at] = attended.astype(bf16)
        grad_query = contract(grad_mixing[h], k_ref[0, :, at], 1, 0) + enter * halves(
            contract(g_ref[0, :, at], jnp.concatenate([high, low], axis=0), 1, 1)
        )
        grad_query_ref[0, :, at] = grad_query.astype(bf16)

    lag = jnp.clip(2 * (2 * z - last) + 3, 0, heads)

    def both_steps(i, carry):
        later_step(i)

        @pl.when(i >= lag)
        def _():
            state_step(jnp.maximum(i - lag, 0))

        return carry

    lax.fori_loop(0, heads, both_steps, 0)

    second[y] = jnp.zeros(second.shape[1:], f32)
    second[y, :, :npos] = contract(rows[...], picks[:npos, :], 1, 1, highest)
    for step in range(1, peers):
        across(second, second_send, second_recv, step).start()

    def part_copy(owner):
        target = owner * stride
        return pltpu.make_async_remote_copy(
            src_ref=pay.at[owner],
            dst_ref=parts.at[member],
            send_sem=parts_send.at[owner],
            recv_sem=parts_recv.at[member],
            device_id={"seq": target // docs, "dp": target % docs},
            device_id_type=MESH,
        )

    def finish_code():
        for step in range(1, peers):
            arrived(second, second_send, second_recv, step)
        sums = second[0]
        for peer in range(1, peers):
            sums = sums + second[peer]
        code_grad = sums[0:4, :npos]
        ahead = sums[4:6, :npos]
        projected = [
            jnp.sum(
                code * ahead[b : b + 1, :] - code_grad * along_own[b : b + 1, :],
                axis=1,
                keepdims=True,
            )
            for b in range(2)
        ]
        back_0 = projected[0] * inverse[0][0] + projected[1] * inverse[1][0]
        back_1 = projected[0] * inverse[0][1] + projected[1] * inverse[1][1]
        weight_part = contract(code_grad, stack[:npos, :], 1, 0, highest)
        rotation_part = (
            contract(code, picks[:npos, :], 1, 0, highest)
            - weight_part
            - back_0 * refusal_ref[0:1, :]
            - back_1 * refusal_ref[1:2, :]
        )
        bias_part = jnp.sum(code_grad, axis=1, keepdims=True)
        width = pay.shape[2]
        for owner in range(owners):
            at = slice(owner * width, (owner + 1) * width)
            pay[owner, 0:4, :] = rotation_part[:, at]
            pay[owner, 4:8, :] = weight_part[:, at]
            pay[owner, 8:12, :] = jnp.broadcast_to(bias_part, (4, width))
            pay[owner, 12:16, :] = jnp.zeros((4, width), f32)

            @pl.when(member == owner * stride)
            def _():
                parts[member] = pay[owner]

            @pl.when(member != owner * stride)
            def _():
                part_copy(owner).start()

        spread_grad = contract(select, code_grad, 1, 1, highest)
        for h in range(heads):
            at = slice(h * size, (h + 1) * size)
            wide = grad_moved[:, at]
            for r in range(4):
                wide = wide + spread_grad[:, r : r + 1] * (
                    weight_ref[r : r + 1, at] - rows[r : r + 1, at]
                )
            grad_value_ref[0, :, at] = wide.astype(bf16)

    along_own = along

    @pl.when(z == last)
    def _():
        finish_code()

    def rest(i, carry):
        state_step(i - lag)
        return carry

    lax.fori_loop(heads, heads + lag, rest, 0)

    @pl.when(z < last)
    def _():
        finish_code()

    mine = member // stride
    owning = lax.rem(member, stride) == 0

    def total_copy(step):
        other = lax.rem(member + step, members)
        return pltpu.make_async_remote_copy(
            src_ref=total.at[mine],
            dst_ref=total.at[mine],
            send_sem=total_send.at[step],
            recv_sem=total_recv.at[mine],
            device_id={"seq": other // docs, "dp": lax.rem(other, docs)},
            device_id_type=MESH,
        )

    def part_arrived(step, carry):
        other = lax.rem(member + step, members)
        pltpu.make_async_remote_copy(
            src_ref=pay.at[0],
            dst_ref=parts.at[other],
            send_sem=parts_send.at[0],
            recv_sem=parts_recv.at[other],
            device_id={"seq": other // docs, "dp": lax.rem(other, docs)},
            device_id_type=MESH,
        ).wait_recv()
        return carry

    def total_start(step, carry):
        total_copy(step).start()
        return carry

    def total_sent(step, carry):
        total_copy(step).wait_send()
        return carry

    @pl.when(owning)
    def _():
        lax.fori_loop(1, members, part_arrived, 0)
        total[mine] = jnp.sum(parts[...], axis=0)
        lax.fori_loop(1, members, total_start, 0)

    width = pay.shape[2]
    for owner in range(owners):

        @pl.when(member != owner * stride)
        def _():
            pltpu.make_async_remote_copy(
                src_ref=total.at[owner],
                dst_ref=total.at[owner],
                send_sem=total_send.at[0],
                recv_sem=total_recv.at[owner],
                device_id={"seq": (owner * stride) // docs, "dp": (owner * stride) % docs},
                device_id_type=MESH,
            ).wait_recv()

    for owner in range(owners):
        at = slice(owner * width, (owner + 1) * width)
        grad_rotation_ref[:, at] = total[owner, 0:4, :]
        grad_weight_ref[:, at] = total[owner, 4:8, :]
    for r in range(4):
        grad_bias_ref[r] = jnp.sum(total[0, 8 + r : 9 + r, 0:1])

    for step in range(1, peers):
        across(first, first_send, first_recv, step).wait_send()
        across(second, second_send, second_recv, step).wait_send()

    def sent(h, carry):
        @pl.when(z < last)
        def _():
            state_copy(h).wait_send()

        @pl.when(z > 0)
        def _():
            later_copy(h).wait_send()

        return carry

    lax.fori_loop(0, heads, sent, 0)
    for owner in range(owners):

        @pl.when(member != owner * stride)
        def _():
            part_copy(owner).wait_send()

    @pl.when(owning)
    def _():
        lax.fori_loop(1, members, total_sent, 0)


def shards(mesh, *arrays):
    (queries, key_rows, values, out_grad, decay_rate, rotation, refusal, weight, bias, positions) = (
        arrays
    )
    seqs, peers, docs = mesh.shape["seq"], mesh.shape["head"], mesh.shape["dp"]
    heads = decay_rate.shape[0]
    group, width = queries.shape[1], queries.shape[2]
    size = width // heads
    npos = positions.shape[1]
    members = seqs * docs
    owners = min(members, width // 128)
    vmem = pl.BlockSpec(memory_space=pltpu.VMEM)
    smem = pl.BlockSpec(memory_space=pltpu.SMEM)
    dma = pltpu.SemaphoreType.DMA
    square = (heads, size, size)
    big = jax.ShapeDtypeStruct(queries.shape, bf16)
    return pl.pallas_call(
        functools.partial(kernel, (seqs, peers, docs, heads, owners)),
        out_shape=(
            big,
            big,
            big,
            big,
            jax.ShapeDtypeStruct(rotation.shape, f32),
            jax.ShapeDtypeStruct(weight.shape, f32),
            jax.ShapeDtypeStruct(bias.shape, f32),
        ),
        in_specs=[vmem, vmem, vmem, vmem, smem, vmem, vmem, vmem, smem, vmem],
        out_specs=(vmem, vmem, vmem, vmem, vmem, vmem, smem),
        scratch_shapes=[
            pltpu.VMEM((npos + 16, width), f32),
            pltpu.VMEM((npos, width), f32),
            pltpu.VMEM((8, width), f32),
            pltpu.VMEM((group, width), bf16),
            pltpu.VMEM((heads, group, group), f32),
            pltpu.VMEM((heads, group, group), bf16),
            pltpu.VMEM((heads, group, group), bf16),
            pltpu.VMEM((group, width), f32),
            pltpu.VMEM(square, f32),
            pltpu.VMEM(square, f32),
            pltpu.VMEM(square, f32),
            pltpu.VMEM(square, f32),
            pltpu.VMEM((peers, 16, 128), f32),
            pltpu.VMEM((peers, 8, 128), f32),
            pltpu.VMEM((owners, 16, width // owners), f32),
            pltpu.VMEM((members, 16, width // owners), f32),
            pltpu.VMEM((owners, 16, width // owners), f32),
            dma((peers,)),
            dma((peers,)),
            dma((peers,)),
            dma((peers,)),
            dma((heads,)),
            dma((heads,)),
            dma((heads,)),
            dma((heads,)),
            dma((owners,)),
            dma((members,)),
            dma((members,)),
            dma((owners,)),
        ],
        compiler_params=pltpu.CompilerParams(
            collective_id=0, has_side_effects=True, vmem_limit_bytes=40 * 1024 * 1024
        ),
    )(queries, key_rows, values, out_grad, decay_rate, rotation, refusal.T, weight, bias, positions)


def solution(mesh):
    return jax.shard_map(
        functools.partial(shards, mesh),
        mesh=mesh,
        in_specs=(
            P("dp", "seq", "head"),
            P("dp", "seq", "head"),
            P("dp", "seq", "head"),
            P("dp", "seq", "head"),
            P("head"),
            P(None, "head"),
            P("head", None),
            P(None, "head"),
            P(),
            P("dp", None),
        ),
        out_specs=(
            P("dp", "seq", "head"),
            P("dp", "seq", "head"),
            P("dp", "seq", "head"),
            P("dp", "seq", "head"),
            P(None, "head"),
            P(None, "head"),
            P(),
        ),
        check_vma=False,
    )
```

```python
import functools
import jax
import jax.numpy as jnp
from jax import lax
from jax.experimental import pallas as pl
from jax.experimental.pallas import tpu as pltpu
from jax.sharding import PartitionSpec as P

highest = lax.Precision.HIGHEST
MESH = pl.DeviceIdType.MESH
f32 = jnp.float32
bf16 = jnp.bfloat16


def contract(a, b, da, db, precision=None):
    return lax.dot_general(
        a, b, (((da,), (db,)), ((), ())), precision=precision, preferred_element_type=f32
    )


def split(x):
    high = x.astype(bf16)
    return high, (x - high.astype(f32)).astype(bf16)


def halves(x):
    n = x.shape[1] // 2
    return x[:, :n] + x[:, n:]


def kernel(
    sizes,
    q_in,
    k_in,
    v_in,
    g_in,
    decay_in,
    rotation_in,
    refusal_in,
    weight_in,
    bias_in,
    positions_in,
    attended_out,
    grad_query_out,
    grad_key_out,
    grad_value_out,
    grad_rotation_out,
    grad_weight_out,
    grad_bias_out,
    attended_ref,
    grad_query_ref,
    grad_key_ref,
    grad_value_ref,
    grad_rotation_ref,
    grad_weight_ref,
    grad_bias_ref,
    store_sem,
    q_ref,
    k_ref,
    v_ref,
    g_ref,
    decay_ref,
    rotation_ref,
    refusal_ref,
    weight_ref,
    bias_ref,
    positions_ref,
    load_sem,
    select_rows,
    inner,
    inner_query,
    stack,
    picks,
    rows,
    moved,
    grad_moved,
    state,
    state_in,
    later,
    later_in,
    first,
    second,
    pay,
    parts,
    total,
    first_send,
    first_recv,
    second_send,
    second_recv,
    state_send,
    state_recv,
    later_send,
    later_recv,
    parts_send,
    parts_recv,
    total_send,
    total_recv,
):
    seqs, peers, docs, heads, owners = sizes
    group = q_ref.shape[1]
    size = q_ref.shape[2] // heads
    npos = positions_ref.shape[1]
    members = seqs * docs
    stride = members // owners
    z, y, c = lax.axis_index("seq"), lax.axis_index("head"), lax.axis_index("dp")
    last = seqs - 1
    member = z * docs + c

    loads = [
        pltpu.make_async_copy(source, target, load_sem.at[i])
        for i, (source, target) in enumerate(
            (
                (v_in, v_ref),
                (positions_in, positions_ref),
                (weight_in, weight_ref),
                (rotation_in, rotation_ref),
                (refusal_in, refusal_ref),
                (decay_in, decay_ref),
                (bias_in, bias_ref),
                (q_in, q_ref),
                (g_in, g_ref),
                (k_in, k_ref),
            )
        )
    ]
    for load in loads:
        load.start()
    stores = [
        pltpu.make_async_copy(source, target, store_sem.at[i])
        for i, (source, target) in enumerate(
            (
                (attended_ref, attended_out),
                (grad_query_ref, grad_query_out),
                (grad_key_ref, grad_key_out),
                (grad_value_ref, grad_value_out),
                (grad_rotation_ref, grad_rotation_out),
                (grad_weight_ref, grad_weight_out),
                (grad_bias_ref, grad_bias_out),
            )
        )
    ]
    barrier = pltpu.get_barrier_semaphore()
    for step in range(1, peers):
        pl.semaphore_signal(
            barrier, inc=1, device_id={"head": lax.rem(y + step, peers)}, device_id_type=MESH
        )

    def greet(step, carry):
        other = lax.rem(member + step, members)
        pl.semaphore_signal(
            barrier,
            inc=1,
            device_id={"seq": other // docs, "dp": lax.rem(other, docs)},
            device_id_type=MESH,
        )
        return carry

    lax.fori_loop(1, members, greet, 0)

    for load in loads[:5]:
        load.wait()
    places = z * group + lax.broadcasted_iota(jnp.int32, (group, npos), 0)
    chosen = places == positions_ref[...]
    select = jnp.where(chosen, 1.0, 0.0)
    turned = select.T
    select_rows[...] = turned.astype(bf16)
    stack[npos:, :] = jnp.zeros((stack.shape[0] - npos, stack.shape[1]), f32)
    picked = contract(select_rows[...], v_ref[0], 1, 0)
    stack[:npos, :] = picked
    stack[npos : npos + 4, :] = weight_ref[...]
    stack[npos + 4 : npos + 8, :] = rotation_ref[...]
    stack[npos + 8 : npos + 10, :] = refusal_ref[...]
    first[y] = jnp.zeros(first.shape[1:], f32)
    first[y, :, : stack.shape[0]] = contract(stack[npos:, :], stack[...], 1, 1, highest)
    pl.semaphore_wait(barrier, peers - 1 + members - 1)

    def across(buffer, send, recv, step):
        other = lax.rem(y + step, peers)
        return pltpu.make_async_remote_copy(
            src_ref=buffer.at[y],
            dst_ref=buffer.at[y],
            send_sem=send.at[step - 1],
            recv_sem=recv.at[y],
            device_id={"head": other},
            device_id_type=MESH,
        )

    def arrived(buffer, send, recv, step):
        other = lax.rem(y + step, peers)
        pltpu.make_async_remote_copy(
            src_ref=buffer.at[other],
            dst_ref=buffer.at[other],
            send_sem=send.at[step - 1],
            recv_sem=recv.at[other],
            device_id={"head": other},
            device_id_type=MESH,
        ).wait_recv()

    for step in range(1, peers):
        across(first, first_send, first_recv, step).start()

    def state_copy(h):
        return pltpu.make_async_remote_copy(
            src_ref=state.at[h],
            dst_ref=state_in.at[h],
            send_sem=state_send.at[h],
            recv_sem=state_recv.at[h],
            device_id={"seq": lax.rem(z + 1, seqs)},
            device_id_type=MESH,
        )

    def later_copy(h):
        return pltpu.make_async_remote_copy(
            src_ref=later.at[h],
            dst_ref=later_in.at[h],
            send_sem=later_send.at[h],
            recv_sem=later_recv.at[h],
            device_id={"seq": lax.rem(z + seqs - 1, seqs)},
            device_id_type=MESH,
        )

    offsets = lax.broadcasted_iota(jnp.int32, (group, size), 0).astype(f32)

    def log_decay(h):
        return jnp.log1p(-jnp.full((1, size), decay_ref[h], f32))

    for load in loads[5:9]:
        load.wait()
    for h in range(heads):
        at = slice(h * size, (h + 1) * size)
        weighted = g_ref[0, :, at].astype(f32) * jnp.exp(offsets * log_decay(h))
        both = jnp.concatenate(split(weighted), axis=1)
        later[h] = halves(contract(q_ref[0, :, at], both, 0, 0))

        @pl.when(z == last)
        def _():
            later_copy(h).start()

    @pl.when(z == last)
    def _():
        later_in[...] = jnp.zeros_like(later_in)

    @pl.when(z == 0)
    def _():
        state_in[...] = jnp.zeros_like(state_in)

    between = lax.broadcasted_iota(jnp.int32, (group, group), 0) - lax.broadcasted_iota(
        jnp.int32, (group, group), 1
    )
    apart = jnp.maximum(between, 0).astype(f32)

    for step in range(1, peers):
        arrived(first, first_send, first_recv, step)
    summed = first[0]
    for peer in range(1, peers):
        summed = summed + first[peer]
    at_ref = npos + 8
    gram = [
        [summed[8 + a : 9 + a, at_ref + b : at_ref + b + 1] for b in range(2)] for a in range(2)
    ]
    determinant = gram[0][0] * gram[1][1] - gram[0][1] * gram[1][0]
    inverse = [
        [gram[1][1] / determinant, -gram[0][1] / determinant],
        [-gram[1][0] / determinant, gram[0][0] / determinant],
    ]
    coupling = [summed[4:8, at_ref + b : at_ref + b + 1] for b in range(2)]
    map_0 = coupling[0] * inverse[0][0] + coupling[1] * inverse[1][0]
    map_1 = coupling[0] * inverse[0][1] + coupling[1] * inverse[1][1]
    rotated = rotation_ref[...] - map_0 * refusal_ref[0:1, :] - map_1 * refusal_ref[1:2, :]
    rows[...] = jnp.zeros_like(rows)
    rows[0:4, :] = rotated
    rows[4:6, :] = refusal_ref[...]
    along = summed[8:10, :npos]
    rank = lax.broadcasted_iota(jnp.int32, (4, npos), 0)
    bias = jnp.zeros((4, npos), f32)
    for r in range(4):
        bias = jnp.where(rank == r, bias_ref[r], bias)
    code = (
        summed[0:4, :npos]
        + bias
        - (summed[4:8, :npos] - map_0 * along[0:1, :] - map_1 * along[1:2, :])
    )
    spread = contract(select, code, 1, 1, highest)
    loads[9].wait()
    for h in range(heads):
        at = slice(h * size, (h + 1) * size)
        value = v_ref[0, :, at].astype(f32)
        shift = spread[:, 0:1] * rows[0:1, at]
        for r in range(1, 4):
            shift = shift + spread[:, r : r + 1] * rows[r : r + 1, at]
        value = (value + shift).astype(bf16)
        moved[:, at] = value
        weighted = value.astype(f32) * jnp.exp((group - 1.0 - offsets) * log_decay(h))
        both = jnp.concatenate(split(weighted), axis=1)
        state[h] = halves(contract(k_ref[0, :, at], both, 0, 0))

        @pl.when(z == 0)
        def _():
            state_copy(h).start()

    def later_step(h):
        at = pl.ds(pl.multiple_of(h * size, size), size)
        decay = log_decay(h)

        @pl.when(z < last)
        def _():
            later_copy(h).wait_recv()

        @pl.when(jnp.logical_and(z > 0, z < last))
        def _():
            later[h] = later[h] + jnp.exp(group * decay) * later_in[h]
            later_copy(h).start()

        high, low = split(later_in[h])
        leave = jnp.exp((group - offsets) * decay)
        table = jnp.where(between >= 0, jnp.exp(apart * decay), 0.0)
        query, key = q_ref[0, :, at], k_ref[0, :, at]
        grad, value = g_ref[0, :, at], moved[:, at]
        mixing = (contract(query, key, 1, 1) * table).astype(bf16)
        mixed = (contract(grad, value, 1, 1) * table).astype(bf16)
        wide = contract(mixing, grad, 0, 0) + leave * halves(
            contract(key, jnp.concatenate([high, low], axis=1), 1, 0)
        )
        grad_moved[:, at] = wide
        picks[:npos, at] = halves(
            contract(select_rows[...], jnp.concatenate(split(wide), axis=1), 1, 0)
        )
        grad_key = contract(mixed, query, 0, 0) + leave * halves(
            contract(value, jnp.concatenate([high, low], axis=0), 1, 1)
        )
        grad_key_ref[0, :, at] = grad_key.astype(bf16)
        inner[:, at] = contract(mixing, value, 1, 0)
        inner_query[:, at] = contract(mixed, key, 1, 0)

    def state_step(h):
        at = pl.ds(pl.multiple_of(h * size, size), size)
        decay = log_decay(h)

        @pl.when(z > 0)
        def _():
            state_copy(h).wait_recv()

        @pl.when(jnp.logical_and(z > 0, z < last))
        def _():
            state[h] = state[h] + jnp.exp(group * decay) * state_in[h]
            state_copy(h).start()

        high, low = split(state_in[h])
        enter = jnp.exp((offsets + 1.0) * decay)
        attended = inner[:, at] + enter * halves(
            contract(q_ref[0, :, at], jnp.concatenate([high, low], axis=1), 1, 0)
        )
        attended_ref[0, :, at] = attended.astype(bf16)
        grad_query = inner_query[:, at] + enter * halves(
            contract(g_ref[0, :, at], jnp.concatenate([high, low], axis=0), 1, 1)
        )
        grad_query_ref[0, :, at] = grad_query.astype(bf16)

    lag = jnp.clip(2 * (2 * z - last) + 3, 0, heads)

    def both_steps(i, carry):
        later_step(i)

        @pl.when(i >= lag)
        def _():
            state_step(jnp.maximum(i - lag, 0))

        return carry

    lax.fori_loop(0, heads, both_steps, 0)

    stores[2].start()

    second[y] = jnp.zeros(second.shape[1:], f32)
    second[y, :, :npos] = contract(rows[...], picks[:npos, :], 1, 1, highest)
    for step in range(1, peers):
        across(second, second_send, second_recv, step).start()

    def part_copy(owner):
        target = owner * stride
        return pltpu.make_async_remote_copy(
            src_ref=pay.at[owner],
            dst_ref=parts.at[member],
            send_sem=parts_send.at[owner],
            recv_sem=parts_recv.at[member],
            device_id={"seq": target // docs, "dp": target % docs},
            device_id_type=MESH,
        )

    def finish_code():
        for step in range(1, peers):
            arrived(second, second_send, second_recv, step)
        sums = second[0]
        for peer in range(1, peers):
            sums = sums + second[peer]
        code_grad = sums[0:4, :npos]
        ahead = sums[4:6, :npos]
        projected = [
            jnp.sum(
                code * ahead[b : b + 1, :] - code_grad * along_own[b : b + 1, :],
                axis=1,
                keepdims=True,
            )
            for b in range(2)
        ]
        back_0 = projected[0] * inverse[0][0] + projected[1] * inverse[1][0]
        back_1 = projected[0] * inverse[0][1] + projected[1] * inverse[1][1]
        weight_part = contract(code_grad, stack[:npos, :], 1, 0, highest)
        rotation_part = (
            contract(code, picks[:npos, :], 1, 0, highest)
            - weight_part
            - back_0 * refusal_ref[0:1, :]
            - back_1 * refusal_ref[1:2, :]
        )
        bias_part = contract(jnp.ones((8, npos), f32), code_grad, 1, 1, highest)
        width = pay.shape[2]
        for owner in range(owners):
            at = slice(owner * width, (owner + 1) * width)
            pay[owner, 0:4, :] = rotation_part[:, at]
            pay[owner, 4:8, :] = weight_part[:, at]
            pay[owner, 8:16, :] = jnp.zeros((8, width), f32)
            pay[owner, 8:16, 0:4] = bias_part

            @pl.when(member == owner * stride)
            def _():
                parts[member] = pay[owner]

            @pl.when(member != owner * stride)
            def _():
                part_copy(owner).start()

        spread_grad = contract(select, code_grad, 1, 1, highest)
        for h in range(heads):
            at = slice(h * size, (h + 1) * size)
            wide = grad_moved[:, at]
            for r in range(4):
                wide = wide + spread_grad[:, r : r + 1] * (
                    weight_ref[r : r + 1, at] - rows[r : r + 1, at]
                )
            grad_value_ref[0, :, at] = wide.astype(bf16)
        stores[3].start()

    along_own = along

    @pl.when(z == last)
    def _():
        finish_code()

    def rest(i, carry):
        state_step(i - lag)
        return carry

    lax.fori_loop(heads, heads + lag, rest, 0)
    stores[0].start()
    stores[1].start()

    @pl.when(z < last)
    def _():
        finish_code()

    mine = member // stride
    owning = lax.rem(member, stride) == 0

    def total_copy(step):
        other = lax.rem(member + step, members)
        return pltpu.make_async_remote_copy(
            src_ref=total.at[mine],
            dst_ref=total.at[mine],
            send_sem=total_send.at[step],
            recv_sem=total_recv.at[mine],
            device_id={"seq": other // docs, "dp": lax.rem(other, docs)},
            device_id_type=MESH,
        )

    def part_arrived(step, carry):
        other = lax.rem(member + step, members)
        pltpu.make_async_remote_copy(
            src_ref=pay.at[0],
            dst_ref=parts.at[other],
            send_sem=parts_send.at[0],
            recv_sem=parts_recv.at[other],
            device_id={"seq": other // docs, "dp": lax.rem(other, docs)},
            device_id_type=MESH,
        ).wait_recv()
        return carry

    def total_start(step, carry):
        total_copy(step).start()
        return carry

    def total_sent(step, carry):
        total_copy(step).wait_send()
        return carry

    @pl.when(owning)
    def _():
        lax.fori_loop(1, members, part_arrived, 0)
        total[mine] = jnp.sum(parts[...], axis=0)
        lax.fori_loop(1, members, total_start, 0)

    width = pay.shape[2]
    for owner in range(owners):

        @pl.when(member != owner * stride)
        def _():
            pltpu.make_async_remote_copy(
                src_ref=total.at[owner],
                dst_ref=total.at[owner],
                send_sem=total_send.at[0],
                recv_sem=total_recv.at[owner],
                device_id={"seq": (owner * stride) // docs, "dp": (owner * stride) % docs},
                device_id_type=MESH,
            ).wait_recv()

    for owner in range(owners):
        at = slice(owner * width, (owner + 1) * width)
        grad_rotation_ref[:, at] = total[owner, 0:4, :]
        grad_weight_ref[:, at] = total[owner, 4:8, :]
    grad_bias_ref[...] = total[0, 8:9, 0:4]
    for i in range(4, 7):
        stores[i].start()

    for i in range(7):
        stores[i].wait()
    for step in range(1, peers):
        across(first, first_send, first_recv, step).wait_send()
        across(second, second_send, second_recv, step).wait_send()

    def sent(h, carry):
        @pl.when(z < last)
        def _():
            state_copy(h).wait_send()

        @pl.when(z > 0)
        def _():
            later_copy(h).wait_send()

        return carry

    lax.fori_loop(0, heads, sent, 0)
    for owner in range(owners):

        @pl.when(member != owner * stride)
        def _():
            part_copy(owner).wait_send()

    @pl.when(owning)
    def _():
        lax.fori_loop(1, members, total_sent, 0)


def store(*refs):
    copies = [
        pltpu.make_async_copy(source, target, refs[14].at[i])
        for i, (source, target) in enumerate(zip(refs[:7], refs[7:14]))
    ]
    for copy in copies:
        copy.start()
    for copy in copies:
        copy.wait()


def shards(mesh, *arrays):
    (queries, key_rows, values, out_grad, decay_rate, rotation, refusal, weight, bias, positions) = (
        arrays
    )
    seqs, peers, docs = mesh.shape["seq"], mesh.shape["head"], mesh.shape["dp"]
    heads = decay_rate.shape[0]
    group, width = queries.shape[1], queries.shape[2]
    size = width // heads
    npos = positions.shape[1]
    members = seqs * docs
    owners = min(members, width // 128)
    limit = 60 * 1024 * 1024
    hbm = pl.BlockSpec(memory_space=pltpu.HBM)
    dma = pltpu.SemaphoreType.DMA
    square = (heads, size, size)
    big = jax.ShapeDtypeStruct(queries.shape, bf16)
    results = pl.pallas_call(
        functools.partial(kernel, (seqs, peers, docs, heads, owners)),
        out_shape=(
            big,
            big,
            big,
            big,
            jax.ShapeDtypeStruct(rotation.shape, f32),
            jax.ShapeDtypeStruct(weight.shape, f32),
            jax.ShapeDtypeStruct((1,) + bias.shape, f32),
        ),
        in_specs=[hbm] * 10,
        out_specs=(hbm,) * 7,
        scratch_shapes=[
            pltpu.VMEM(queries.shape, bf16),
            pltpu.VMEM(queries.shape, bf16),
            pltpu.VMEM(queries.shape, bf16),
            pltpu.VMEM(queries.shape, bf16),
            pltpu.VMEM(rotation.shape, f32),
            pltpu.VMEM(weight.shape, f32),
            pltpu.VMEM((1,) + bias.shape, f32),
            dma((7,)),
            pltpu.VMEM(queries.shape, bf16),
            pltpu.VMEM(queries.shape, bf16),
            pltpu.VMEM(queries.shape, bf16),
            pltpu.VMEM(queries.shape, bf16),
            pltpu.SMEM(decay_rate.shape, f32),
            pltpu.VMEM(rotation.shape, f32),
            pltpu.VMEM((2, width), f32),
            pltpu.VMEM(weight.shape, f32),
            pltpu.SMEM(bias.shape, f32),
            pltpu.VMEM(positions.shape, jnp.int32),
            dma((10,)),
            pltpu.VMEM((npos, group), bf16),
            pltpu.VMEM((group, width), f32),
            pltpu.VMEM((group, width), f32),
            pltpu.VMEM((npos + 16, width), f32),
            pltpu.VMEM((npos, width), f32),
            pltpu.VMEM((8, width), f32),
            pltpu.VMEM((group, width), bf16),
            pltpu.VMEM((group, width), f32),
            pltpu.VMEM(square, f32),
            pltpu.VMEM(square, f32),
            pltpu.VMEM(square, f32),
            pltpu.VMEM(square, f32),
            pltpu.VMEM((peers, 16, 128), f32),
            pltpu.VMEM((peers, 8, 128), f32),
            pltpu.VMEM((owners, 16, width // owners), f32),
            pltpu.VMEM((members, 16, width // owners), f32),
            pltpu.VMEM((owners, 16, width // owners), f32),
            dma((peers,)),
            dma((peers,)),
            dma((peers,)),
            dma((peers,)),
            dma((heads,)),
            dma((heads,)),
            dma((heads,)),
            dma((heads,)),
            dma((owners,)),
            dma((members,)),
            dma((members,)),
            dma((owners,)),
        ],
        compiler_params=pltpu.CompilerParams(
            collective_id=0, has_side_effects=True, vmem_limit_bytes=limit
        ),
    )(queries, key_rows, values, out_grad, decay_rate, rotation, refusal.T, weight, bias, positions)
    results = pl.pallas_call(
        store,
        out_shape=tuple(jax.ShapeDtypeStruct(x.shape, x.dtype) for x in results),
        in_specs=[hbm] * 7,
        out_specs=(hbm,) * 7,
        scratch_shapes=[dma((7,))],
        compiler_params=pltpu.CompilerParams(vmem_limit_bytes=limit),
    )(*results)
    return results[:6] + (results[6].reshape(bias.shape),)


def solution(mesh):
    return jax.shard_map(
        functools.partial(shards, mesh),
        mesh=mesh,
        in_specs=(
            P("dp", "seq", "head"),
            P("dp", "seq", "head"),
            P("dp", "seq", "head"),
            P("dp", "seq", "head"),
            P("head"),
            P(None, "head"),
            P("head", None),
            P(None, "head"),
            P(),
            P("dp", None),
        ),
        out_specs=(
            P("dp", "seq", "head"),
            P("dp", "seq", "head"),
            P("dp", "seq", "head"),
            P("dp", "seq", "head"),
            P(None, "head"),
            P(None, "head"),
            P(),
        ),
        check_vma=False,
    )
```

```python
import functools
import jax
import jax.numpy as jnp
from jax import lax
from jax.experimental import pallas as pl
from jax.experimental.pallas import tpu as pltpu
from jax.sharding import PartitionSpec as P

highest = lax.Precision.HIGHEST
MESH = pl.DeviceIdType.MESH
f32 = jnp.float32
bf16 = jnp.bfloat16


def contract(a, b, da, db, precision=None):
    return lax.dot_general(
        a, b, (((da,), (db,)), ((), ())), precision=precision, preferred_element_type=f32
    )


def split(x):
    high = x.astype(bf16)
    return high, (x - high.astype(f32)).astype(bf16)


def halves(x):
    n = x.shape[1] // 2
    return x[:, :n] + x[:, n:]


def kernel(
    sizes,
    q_in,
    k_in,
    v_in,
    g_in,
    decay_in,
    rotation_in,
    refusal_in,
    weight_in,
    bias_in,
    positions_in,
    attended_out,
    grad_query_out,
    grad_key_out,
    grad_value_out,
    grad_rotation_out,
    grad_weight_out,
    grad_bias_out,
    attended_ref,
    grad_query_ref,
    grad_key_ref,
    grad_value_ref,
    grad_rotation_ref,
    grad_weight_ref,
    grad_bias_ref,
    store_sem,
    q_ref,
    k_ref,
    v_ref,
    g_ref,
    decay_ref,
    rotation_ref,
    refusal_ref,
    weight_ref,
    bias_ref,
    positions_ref,
    load_sem,
    select_rows,
    inner,
    inner_query,
    stack,
    picks,
    rows,
    moved,
    grad_moved,
    state,
    state_in,
    later,
    later_in,
    first,
    second,
    pay,
    parts,
    total,
    first_send,
    first_recv,
    second_send,
    second_recv,
    state_send,
    state_recv,
    later_send,
    later_recv,
    parts_send,
    parts_recv,
    total_send,
    total_recv,
):
    seqs, peers, docs, heads, owners = sizes
    group = q_ref.shape[1]
    size = q_ref.shape[2] // heads
    npos = positions_ref.shape[1]
    members = seqs * docs
    stride = members // owners
    z, y, c = lax.axis_index("seq"), lax.axis_index("head"), lax.axis_index("dp")
    last = seqs - 1
    member = z * docs + c

    loads = [
        pltpu.make_async_copy(source, target, load_sem.at[i])
        for i, (source, target) in enumerate(
            (
                (decay_in, decay_ref),
                (q_in, q_ref),
                (g_in, g_ref),
                (v_in, v_ref),
                (positions_in, positions_ref),
                (weight_in, weight_ref),
                (rotation_in, rotation_ref),
                (refusal_in, refusal_ref),
                (bias_in, bias_ref),
                (k_in, k_ref),
            )
        )
    ]
    for load in loads:
        load.start()
    stores = [
        pltpu.make_async_copy(source, target, store_sem.at[i])
        for i, (source, target) in enumerate(
            (
                (attended_ref, attended_out),
                (grad_query_ref, grad_query_out),
                (grad_key_ref, grad_key_out),
                (grad_value_ref, grad_value_out),
                (grad_rotation_ref, grad_rotation_out),
                (grad_weight_ref, grad_weight_out),
                (grad_bias_ref, grad_bias_out),
            )
        )
    ]
    barrier = pltpu.get_barrier_semaphore()
    for step in range(1, peers):
        pl.semaphore_signal(
            barrier, inc=1, device_id={"head": lax.rem(y + step, peers)}, device_id_type=MESH
        )

    def greet(step, carry):
        other = lax.rem(member + step, members)
        pl.semaphore_signal(
            barrier,
            inc=1,
            device_id={"seq": other // docs, "dp": lax.rem(other, docs)},
            device_id_type=MESH,
        )
        return carry

    lax.fori_loop(1, members, greet, 0)

    def across(buffer, send, recv, step):
        other = lax.rem(y + step, peers)
        return pltpu.make_async_remote_copy(
            src_ref=buffer.at[y],
            dst_ref=buffer.at[y],
            send_sem=send.at[step - 1],
            recv_sem=recv.at[y],
            device_id={"head": other},
            device_id_type=MESH,
        )

    def arrived(buffer, send, recv, step):
        other = lax.rem(y + step, peers)
        pltpu.make_async_remote_copy(
            src_ref=buffer.at[other],
            dst_ref=buffer.at[other],
            send_sem=send.at[step - 1],
            recv_sem=recv.at[other],
            device_id={"head": other},
            device_id_type=MESH,
        ).wait_recv()

    def state_copy(h):
        return pltpu.make_async_remote_copy(
            src_ref=state.at[h],
            dst_ref=state_in.at[h],
            send_sem=state_send.at[h],
            recv_sem=state_recv.at[h],
            device_id={"seq": lax.rem(z + 1, seqs)},
            device_id_type=MESH,
        )

    def later_copy(h):
        return pltpu.make_async_remote_copy(
            src_ref=later.at[h],
            dst_ref=later_in.at[h],
            send_sem=later_send.at[h],
            recv_sem=later_recv.at[h],
            device_id={"seq": lax.rem(z + seqs - 1, seqs)},
            device_id_type=MESH,
        )

    offsets = lax.broadcasted_iota(jnp.int32, (group, size), 0).astype(f32)

    def log_decay(h):
        return jnp.log1p(-jnp.full((1, size), decay_ref[h], f32))

    for load in loads[:3]:
        load.wait()
    for h in range(heads):
        at = slice(h * size, (h + 1) * size)
        weighted = g_ref[0, :, at].astype(f32) * jnp.exp(offsets * log_decay(h))
        both = jnp.concatenate(split(weighted), axis=1)
        later[h] = halves(contract(q_ref[0, :, at], both, 0, 0))
        if h == 0:
            pl.semaphore_wait(barrier, peers - 1 + members - 1)

        @pl.when(z == last)
        def _():
            later_copy(h).start()

    for load in loads[3:8]:
        load.wait()
    places = z * group + lax.broadcasted_iota(jnp.int32, (group, npos), 0)
    chosen = places == positions_ref[...]
    select = jnp.where(chosen, 1.0, 0.0)
    turned = select.T
    select_rows[...] = turned.astype(bf16)
    stack[npos:, :] = jnp.zeros((stack.shape[0] - npos, stack.shape[1]), f32)
    picked = contract(select_rows[...], v_ref[0], 1, 0)
    stack[:npos, :] = picked
    stack[npos : npos + 4, :] = weight_ref[...]
    stack[npos + 4 : npos + 8, :] = rotation_ref[...]
    stack[npos + 8 : npos + 10, :] = refusal_ref[...]
    first[y] = jnp.zeros(first.shape[1:], f32)
    first[y, :, : stack.shape[0]] = contract(stack[npos:, :], stack[...], 1, 1, highest)
    for step in range(1, peers):
        across(first, first_send, first_recv, step).start()

    @pl.when(z == last)
    def _():
        later_in[...] = jnp.zeros_like(later_in)

    @pl.when(z == 0)
    def _():
        state_in[...] = jnp.zeros_like(state_in)

    between = lax.broadcasted_iota(jnp.int32, (group, group), 0) - lax.broadcasted_iota(
        jnp.int32, (group, group), 1
    )
    apart = jnp.maximum(between, 0).astype(f32)

    loads[8].wait()
    for step in range(1, peers):
        arrived(first, first_send, first_recv, step)
    summed = first[0]
    for peer in range(1, peers):
        summed = summed + first[peer]
    at_ref = npos + 8
    gram = [
        [summed[8 + a : 9 + a, at_ref + b : at_ref + b + 1] for b in range(2)] for a in range(2)
    ]
    determinant = gram[0][0] * gram[1][1] - gram[0][1] * gram[1][0]
    inverse = [
        [gram[1][1] / determinant, -gram[0][1] / determinant],
        [-gram[1][0] / determinant, gram[0][0] / determinant],
    ]
    coupling = [summed[4:8, at_ref + b : at_ref + b + 1] for b in range(2)]
    map_0 = coupling[0] * inverse[0][0] + coupling[1] * inverse[1][0]
    map_1 = coupling[0] * inverse[0][1] + coupling[1] * inverse[1][1]
    rotated = rotation_ref[...] - map_0 * refusal_ref[0:1, :] - map_1 * refusal_ref[1:2, :]
    rows[...] = jnp.zeros_like(rows)
    rows[0:4, :] = rotated
    rows[4:6, :] = refusal_ref[...]
    along = summed[8:10, :npos]
    rank = lax.broadcasted_iota(jnp.int32, (4, npos), 0)
    bias = jnp.zeros((4, npos), f32)
    for r in range(4):
        bias = jnp.where(rank == r, bias_ref[r], bias)
    code = (
        summed[0:4, :npos]
        + bias
        - (summed[4:8, :npos] - map_0 * along[0:1, :] - map_1 * along[1:2, :])
    )
    spread = contract(select, code, 1, 1, highest)
    loads[9].wait()

    def later_forward(h, carry):
        @pl.when(z < last)
        def _():
            later_copy(h).wait_recv()

        @pl.when(jnp.logical_and(z > 0, z < last))
        def _():
            later[h] = later[h] + jnp.exp(group * log_decay(h)) * later_in[h]
            later_copy(h).start()

        return carry

    most = min(4, heads)
    ahead_count = jnp.where(z < last, jnp.clip(most - 2 * (last - 1 - z), 0, most), 0)
    soon = ahead_count // 2
    lax.fori_loop(0, soon, later_forward, 0)
    for h in range(heads):
        at = slice(h * size, (h + 1) * size)
        value = v_ref[0, :, at].astype(f32)
        shift = spread[:, 0:1] * rows[0:1, at]
        for r in range(1, 4):
            shift = shift + spread[:, r : r + 1] * rows[r : r + 1, at]
        value = (value + shift).astype(bf16)
        moved[:, at] = value
        weighted = value.astype(f32) * jnp.exp((group - 1.0 - offsets) * log_decay(h))
        both = jnp.concatenate(split(weighted), axis=1)
        state[h] = halves(contract(k_ref[0, :, at], both, 0, 0))

        @pl.when(z == 0)
        def _():
            state_copy(h).start()

    lax.fori_loop(soon, ahead_count, later_forward, 0)

    def later_step(h):
        at = pl.ds(pl.multiple_of(h * size, size), size)
        decay = log_decay(h)

        @pl.when(h + ahead_count < heads)
        def _():
            later_forward(jnp.minimum(h + ahead_count, heads - 1), 0)

        high, low = split(later_in[h])
        leave = jnp.exp((group - offsets) * decay)
        table = jnp.where(between >= 0, jnp.exp(apart * decay), 0.0)
        query, key = q_ref[0, :, at], k_ref[0, :, at]
        grad, value = g_ref[0, :, at], moved[:, at]
        mixing = (contract(query, key, 1, 1) * table).astype(bf16)
        mixed = (contract(grad, value, 1, 1) * table).astype(bf16)
        wide = contract(mixing, grad, 0, 0) + leave * halves(
            contract(key, jnp.concatenate([high, low], axis=1), 1, 0)
        )
        grad_moved[:, at] = wide
        picks[:npos, at] = halves(
            contract(select_rows[...], jnp.concatenate(split(wide), axis=1), 1, 0)
        )
        grad_key = contract(mixed, query, 0, 0) + leave * halves(
            contract(value, jnp.concatenate([high, low], axis=0), 1, 1)
        )
        grad_key_ref[0, :, at] = grad_key.astype(bf16)
        inner[:, at] = contract(mixing, value, 1, 0)
        inner_query[:, at] = contract(mixed, key, 1, 0)

    def state_step(h):
        at = pl.ds(pl.multiple_of(h * size, size), size)
        decay = log_decay(h)

        @pl.when(z > 0)
        def _():
            state_copy(h).wait_recv()

        @pl.when(jnp.logical_and(z > 0, z < last))
        def _():
            state[h] = state[h] + jnp.exp(group * decay) * state_in[h]
            state_copy(h).start()

        high, low = split(state_in[h])
        enter = jnp.exp((offsets + 1.0) * decay)
        attended = inner[:, at] + enter * halves(
            contract(q_ref[0, :, at], jnp.concatenate([high, low], axis=1), 1, 0)
        )
        attended_ref[0, :, at] = attended.astype(bf16)
        grad_query = inner_query[:, at] + enter * halves(
            contract(g_ref[0, :, at], jnp.concatenate([high, low], axis=0), 1, 1)
        )
        grad_query_ref[0, :, at] = grad_query.astype(bf16)

    lag = jnp.clip(2 * (2 * z - last) + 3, 1, heads)

    def both_steps(i, carry):
        later_step(i)

        @pl.when(i >= lag)
        def _():
            state_step(jnp.maximum(i - lag, 0))

        return carry

    lax.fori_loop(0, heads, both_steps, 0)

    stores[2].start()

    second[y] = jnp.zeros(second.shape[1:], f32)
    second[y, :, :npos] = contract(rows[...], picks[:npos, :], 1, 1, highest)
    for step in range(1, peers):
        across(second, second_send, second_recv, step).start()

    def part_copy(owner):
        target = owner * stride
        return pltpu.make_async_remote_copy(
            src_ref=pay.at[owner],
            dst_ref=parts.at[member],
            send_sem=parts_send.at[owner],
            recv_sem=parts_recv.at[member],
            device_id={"seq": target // docs, "dp": target % docs},
            device_id_type=MESH,
        )

    def finish_code():
        for step in range(1, peers):
            arrived(second, second_send, second_recv, step)
        sums = second[0]
        for peer in range(1, peers):
            sums = sums + second[peer]
        code_grad = sums[0:4, :npos]
        ahead = sums[4:6, :npos]
        projected = [
            jnp.sum(
                code * ahead[b : b + 1, :] - code_grad * along_own[b : b + 1, :],
                axis=1,
                keepdims=True,
            )
            for b in range(2)
        ]
        back_0 = projected[0] * inverse[0][0] + projected[1] * inverse[1][0]
        back_1 = projected[0] * inverse[0][1] + projected[1] * inverse[1][1]
        weight_part = contract(code_grad, stack[:npos, :], 1, 0, highest)
        rotation_part = (
            contract(code, picks[:npos, :], 1, 0, highest)
            - weight_part
            - back_0 * refusal_ref[0:1, :]
            - back_1 * refusal_ref[1:2, :]
        )
        bias_part = contract(jnp.ones((8, npos), f32), code_grad, 1, 1, highest)
        width = pay.shape[2]
        for owner in range(owners):
            at = slice(owner * width, (owner + 1) * width)
            pay[owner, 0:4, :] = rotation_part[:, at]
            pay[owner, 4:8, :] = weight_part[:, at]
            pay[owner, 8:16, :] = jnp.zeros((8, width), f32)
            pay[owner, 8:16, 0:4] = bias_part

            @pl.when(member == owner * stride)
            def _():
                parts[member] = pay[owner]

            @pl.when(member != owner * stride)
            def _():
                part_copy(owner).start()

        spread_grad = contract(select, code_grad, 1, 1, highest)
        for h in range(heads):
            at = slice(h * size, (h + 1) * size)
            wide = grad_moved[:, at]
            for r in range(4):
                wide = wide + spread_grad[:, r : r + 1] * (
                    weight_ref[r : r + 1, at] - rows[r : r + 1, at]
                )
            grad_value_ref[0, :, at] = wide.astype(bf16)
        stores[3].start()

    along_own = along

    @pl.when(z == last)
    def _():
        finish_code()

    def rest(i, carry):
        state_step(i - lag)
        return carry

    lax.fori_loop(heads, heads + lag, rest, 0)
    stores[0].start()
    stores[1].start()

    @pl.when(z < last)
    def _():
        finish_code()

    mine = member // stride
    owning = lax.rem(member, stride) == 0

    def total_copy(step):
        other = lax.rem(member + step, members)
        return pltpu.make_async_remote_copy(
            src_ref=total.at[mine],
            dst_ref=total.at[mine],
            send_sem=total_send.at[step],
            recv_sem=total_recv.at[mine],
            device_id={"seq": other // docs, "dp": lax.rem(other, docs)},
            device_id_type=MESH,
        )

    def part_arrived(step, carry):
        other = lax.rem(member + step, members)
        pltpu.make_async_remote_copy(
            src_ref=pay.at[0],
            dst_ref=parts.at[other],
            send_sem=parts_send.at[0],
            recv_sem=parts_recv.at[other],
            device_id={"seq": other // docs, "dp": lax.rem(other, docs)},
            device_id_type=MESH,
        ).wait_recv()
        return carry

    def total_start(step, carry):
        total_copy(step).start()
        return carry

    def total_sent(step, carry):
        total_copy(step).wait_send()
        return carry

    @pl.when(owning)
    def _():
        lax.fori_loop(1, members, part_arrived, 0)
        total[mine] = jnp.sum(parts[...], axis=0)
        lax.fori_loop(1, members, total_start, 0)

    width = pay.shape[2]
    for owner in range(owners):

        @pl.when(member != owner * stride)
        def _():
            pltpu.make_async_remote_copy(
                src_ref=total.at[owner],
                dst_ref=total.at[owner],
                send_sem=total_send.at[0],
                recv_sem=total_recv.at[owner],
                device_id={"seq": (owner * stride) // docs, "dp": (owner * stride) % docs},
                device_id_type=MESH,
            ).wait_recv()

    for owner in range(owners):
        at = slice(owner * width, (owner + 1) * width)
        grad_rotation_ref[:, at] = total[owner, 0:4, :]
        grad_weight_ref[:, at] = total[owner, 4:8, :]
    grad_bias_ref[...] = total[0, 8:9, 0:4]
    for i in range(4, 7):
        stores[i].start()

    for i in range(7):
        stores[i].wait()
    for step in range(1, peers):
        across(first, first_send, first_recv, step).wait_send()
        across(second, second_send, second_recv, step).wait_send()

    def sent(h, carry):
        @pl.when(z < last)
        def _():
            state_copy(h).wait_send()

        @pl.when(z > 0)
        def _():
            later_copy(h).wait_send()

        return carry

    lax.fori_loop(0, heads, sent, 0)
    for owner in range(owners):

        @pl.when(member != owner * stride)
        def _():
            part_copy(owner).wait_send()

    @pl.when(owning)
    def _():
        lax.fori_loop(1, members, total_sent, 0)


def store(*refs):
    sources, targets, held, sems = refs[:7], refs[7:14], refs[14:21], refs[21]
    fetches = [pltpu.make_async_copy(sources[i], held[i], sems.at[0, i]) for i in range(7)]
    copies = [pltpu.make_async_copy(held[i], targets[i], sems.at[1, i]) for i in range(7)]
    for fetch in fetches:
        fetch.start()
    for fetch, copy in zip(fetches, copies):
        fetch.wait()
        copy.start()
    for copy in copies:
        copy.wait()


def shards(mesh, *arrays):
    (queries, key_rows, values, out_grad, decay_rate, rotation, refusal, weight, bias, positions) = (
        arrays
    )
    seqs, peers, docs = mesh.shape["seq"], mesh.shape["head"], mesh.shape["dp"]
    heads = decay_rate.shape[0]
    group, width = queries.shape[1], queries.shape[2]
    size = width // heads
    npos = positions.shape[1]
    members = seqs * docs
    owners = min(members, width // 128)
    limit = 60 * 1024 * 1024
    hbm = pl.BlockSpec(memory_space=pltpu.HBM)
    dma = pltpu.SemaphoreType.DMA
    square = (heads, size, size)
    big = jax.ShapeDtypeStruct(queries.shape, bf16)
    results = pl.pallas_call(
        functools.partial(kernel, (seqs, peers, docs, heads, owners)),
        out_shape=(
            big,
            big,
            big,
            big,
            jax.ShapeDtypeStruct(rotation.shape, f32),
            jax.ShapeDtypeStruct(weight.shape, f32),
            jax.ShapeDtypeStruct((1,) + bias.shape, f32),
        ),
        in_specs=[hbm] * 10,
        out_specs=(hbm,) * 7,
        scratch_shapes=[
            pltpu.VMEM(queries.shape, bf16),
            pltpu.VMEM(queries.shape, bf16),
            pltpu.VMEM(queries.shape, bf16),
            pltpu.VMEM(queries.shape, bf16),
            pltpu.VMEM(rotation.shape, f32),
            pltpu.VMEM(weight.shape, f32),
            pltpu.VMEM((1,) + bias.shape, f32),
            dma((7,)),
            pltpu.VMEM(queries.shape, bf16),
            pltpu.VMEM(queries.shape, bf16),
            pltpu.VMEM(queries.shape, bf16),
            pltpu.VMEM(queries.shape, bf16),
            pltpu.SMEM(decay_rate.shape, f32),
            pltpu.VMEM(rotation.shape, f32),
            pltpu.VMEM((2, width), f32),
            pltpu.VMEM(weight.shape, f32),
            pltpu.SMEM(bias.shape, f32),
            pltpu.VMEM(positions.shape, jnp.int32),
            dma((10,)),
            pltpu.VMEM((npos, group), bf16),
            pltpu.VMEM((group, width), f32),
            pltpu.VMEM((group, width), f32),
            pltpu.VMEM((npos + 16, width), f32),
            pltpu.VMEM((npos, width), f32),
            pltpu.VMEM((8, width), f32),
            pltpu.VMEM((group, width), bf16),
            pltpu.VMEM((group, width), f32),
            pltpu.VMEM(square, f32),
            pltpu.VMEM(square, f32),
            pltpu.VMEM(square, f32),
            pltpu.VMEM(square, f32),
            pltpu.VMEM((peers, 16, 128), f32),
            pltpu.VMEM((peers, 8, 128), f32),
            pltpu.VMEM((owners, 16, width // owners), f32),
            pltpu.VMEM((members, 16, width // owners), f32),
            pltpu.VMEM((owners, 16, width // owners), f32),
            dma((peers,)),
            dma((peers,)),
            dma((peers,)),
            dma((peers,)),
            dma((heads,)),
            dma((heads,)),
            dma((heads,)),
            dma((heads,)),
            dma((owners,)),
            dma((members,)),
            dma((members,)),
            dma((owners,)),
        ],
        compiler_params=pltpu.CompilerParams(
            collective_id=0, has_side_effects=True, vmem_limit_bytes=limit
        ),
    )(queries, key_rows, values, out_grad, decay_rate, rotation, refusal.T, weight, bias, positions)
    results = pl.pallas_call(
        store,
        out_shape=tuple(jax.ShapeDtypeStruct(x.shape, x.dtype) for x in results),
        in_specs=[hbm] * 7,
        out_specs=(hbm,) * 7,
        scratch_shapes=[pltpu.VMEM(x.shape, x.dtype) for x in results] + [dma((2, 7))],
        compiler_params=pltpu.CompilerParams(vmem_limit_bytes=limit),
    )(*results)
    return results[:6] + (results[6].reshape(bias.shape),)


def solution(mesh):
    return jax.shard_map(
        functools.partial(shards, mesh),
        mesh=mesh,
        in_specs=(
            P("dp", "seq", "head"),
            P("dp", "seq", "head"),
            P("dp", "seq", "head"),
            P("dp", "seq", "head"),
            P("head"),
            P(None, "head"),
            P("head", None),
            P(None, "head"),
            P(),
            P("dp", None),
        ),
        out_specs=(
            P("dp", "seq", "head"),
            P("dp", "seq", "head"),
            P("dp", "seq", "head"),
            P("dp", "seq", "head"),
            P(None, "head"),
            P(None, "head"),
            P(),
        ),
        check_vma=False,
    )
```

```python
import functools
import jax
import jax.numpy as jnp
from jax import lax
from jax.experimental import pallas as pl
from jax.experimental.pallas import tpu as pltpu
from jax.sharding import PartitionSpec as P

highest = lax.Precision.HIGHEST
MESH = pl.DeviceIdType.MESH
f32 = jnp.float32
bf16 = jnp.bfloat16


def contract(a, b, da, db, precision=None):
    return lax.dot_general(
        a, b, (((da,), (db,)), ((), ())), precision=precision, preferred_element_type=f32
    )


def split(x):
    high = x.astype(bf16)
    return high, (x - high.astype(f32)).astype(bf16)


def halves(x):
    n = x.shape[1] // 2
    return x[:, :n] + x[:, n:]


def kernel(
    sizes,
    q_in,
    k_in,
    v_in,
    g_in,
    decay_in,
    rotation_in,
    refusal_in,
    weight_in,
    bias_in,
    positions_in,
    attended_out,
    grad_query_out,
    grad_key_out,
    grad_value_out,
    grad_rotation_out,
    grad_weight_out,
    grad_bias_out,
    attended_ref,
    grad_query_ref,
    grad_key_ref,
    grad_value_ref,
    grad_rotation_ref,
    grad_weight_ref,
    grad_bias_ref,
    store_sem,
    q_ref,
    k_ref,
    v_ref,
    g_ref,
    decay_ref,
    rotation_ref,
    refusal_ref,
    weight_ref,
    bias_ref,
    positions_ref,
    load_sem,
    select_rows,
    inner,
    inner_query,
    inner_key,
    stack,
    picks,
    rows,
    moved,
    grad_moved,
    state,
    state_in,
    later,
    later_in,
    first,
    second,
    pay,
    parts,
    total,
    first_send,
    first_recv,
    second_send,
    second_recv,
    state_send,
    state_recv,
    later_send,
    later_recv,
    parts_send,
    parts_recv,
    total_send,
    total_recv,
):
    seqs, peers, docs, heads, owners = sizes
    group = q_ref.shape[1]
    size = q_ref.shape[2] // heads
    npos = positions_ref.shape[1]
    members = seqs * docs
    stride = members // owners
    z, y, c = lax.axis_index("seq"), lax.axis_index("head"), lax.axis_index("dp")
    last = seqs - 1
    member = z * docs + c

    loads = [
        pltpu.make_async_copy(source, target, load_sem.at[i])
        for i, (source, target) in enumerate(
            (
                (v_in, v_ref),
                (positions_in, positions_ref),
                (weight_in, weight_ref),
                (rotation_in, rotation_ref),
                (refusal_in, refusal_ref),
                (q_in, q_ref),
                (g_in, g_ref),
                (decay_in, decay_ref),
                (bias_in, bias_ref),
                (k_in, k_ref),
            )
        )
    ]
    for load in loads:
        load.start()
    stores = [
        pltpu.make_async_copy(source, target, store_sem.at[i])
        for i, (source, target) in enumerate(
            (
                (attended_ref, attended_out),
                (grad_query_ref, grad_query_out),
                (grad_key_ref, grad_key_out),
                (grad_value_ref, grad_value_out),
                (grad_rotation_ref, grad_rotation_out),
                (grad_weight_ref, grad_weight_out),
                (grad_bias_ref, grad_bias_out),
            )
        )
    ]
    barrier = pltpu.get_barrier_semaphore()
    for step in range(1, peers):
        pl.semaphore_signal(
            barrier, inc=1, device_id={"head": lax.rem(y + step, peers)}, device_id_type=MESH
        )

    def greet(step, carry):
        other = lax.rem(member + step, members)
        pl.semaphore_signal(
            barrier,
            inc=1,
            device_id={"seq": other // docs, "dp": lax.rem(other, docs)},
            device_id_type=MESH,
        )
        return carry

    lax.fori_loop(1, members, greet, 0)

    def across(buffer, send, recv, step):
        other = lax.rem(y + step, peers)
        return pltpu.make_async_remote_copy(
            src_ref=buffer.at[y],
            dst_ref=buffer.at[y],
            send_sem=send.at[step - 1],
            recv_sem=recv.at[y],
            device_id={"head": other},
            device_id_type=MESH,
        )

    def arrived(buffer, send, recv, step):
        other = lax.rem(y + step, peers)
        pltpu.make_async_remote_copy(
            src_ref=buffer.at[other],
            dst_ref=buffer.at[other],
            send_sem=send.at[step - 1],
            recv_sem=recv.at[other],
            device_id={"head": other},
            device_id_type=MESH,
        ).wait_recv()

    def state_copy(h):
        return pltpu.make_async_remote_copy(
            src_ref=state.at[h],
            dst_ref=state_in.at[h],
            send_sem=state_send.at[h],
            recv_sem=state_recv.at[h],
            device_id={"seq": lax.rem(z + 1, seqs)},
            device_id_type=MESH,
        )

    def later_copy(h):
        return pltpu.make_async_remote_copy(
            src_ref=later.at[h],
            dst_ref=later_in.at[h],
            send_sem=later_send.at[h],
            recv_sem=later_recv.at[h],
            device_id={"seq": lax.rem(z + seqs - 1, seqs)},
            device_id_type=MESH,
        )

    offsets = lax.broadcasted_iota(jnp.int32, (group, size), 0).astype(f32)

    def log_decay(h):
        return jnp.log1p(-jnp.full((1, size), decay_ref[h], f32))

    for load in loads[:5]:
        load.wait()
    places = z * group + lax.broadcasted_iota(jnp.int32, (group, npos), 0)
    chosen = places == positions_ref[...]
    select = jnp.where(chosen, 1.0, 0.0)
    turned = select.T
    select_rows[...] = turned.astype(bf16)
    stack[npos:, :] = jnp.zeros((stack.shape[0] - npos, stack.shape[1]), f32)
    picked = contract(select_rows[...], v_ref[0], 1, 0)
    stack[:npos, :] = picked
    stack[npos : npos + 4, :] = weight_ref[...]
    stack[npos + 4 : npos + 8, :] = rotation_ref[...]
    stack[npos + 8 : npos + 10, :] = refusal_ref[...]
    first[y] = jnp.zeros(first.shape[1:], f32)
    first[y, :, : stack.shape[0]] = contract(stack[npos:, :], stack[...], 1, 1, highest)
    pl.semaphore_wait(barrier, peers - 1 + members - 1)
    for step in range(1, peers):
        across(first, first_send, first_recv, step).start()

    for load in loads[5:8]:
        load.wait()

    def own_later(h):
        at = slice(h * size, (h + 1) * size)
        weighted = g_ref[0, :, at].astype(f32) * jnp.exp(offsets * log_decay(h))
        both = jnp.concatenate(split(weighted), axis=1)
        later[h] = halves(contract(q_ref[0, :, at], both, 0, 0))

    own_later(0)

    @pl.when(z == last)
    def _():
        later_copy(0).start()

    for h in range(1, heads):
        own_later(h)

    @pl.when(z == last)
    def _():
        for h in range(1, heads):
            later_copy(h).start()

    @pl.when(z == last)
    def _():
        later_in[...] = jnp.zeros_like(later_in)

    @pl.when(z == 0)
    def _():
        state_in[...] = jnp.zeros_like(state_in)

    between = lax.broadcasted_iota(jnp.int32, (group, group), 0) - lax.broadcasted_iota(
        jnp.int32, (group, group), 1
    )
    apart = jnp.maximum(between, 0).astype(f32)

    loads[8].wait()
    for step in range(1, peers):
        arrived(first, first_send, first_recv, step)
    summed = first[0]
    for peer in range(1, peers):
        summed = summed + first[peer]
    at_ref = npos + 8
    gram = [
        [summed[8 + a : 9 + a, at_ref + b : at_ref + b + 1] for b in range(2)] for a in range(2)
    ]
    determinant = gram[0][0] * gram[1][1] - gram[0][1] * gram[1][0]
    inverse = [
        [gram[1][1] / determinant, -gram[0][1] / determinant],
        [-gram[1][0] / determinant, gram[0][0] / determinant],
    ]
    coupling = [summed[4:8, at_ref + b : at_ref + b + 1] for b in range(2)]
    map_0 = coupling[0] * inverse[0][0] + coupling[1] * inverse[1][0]
    map_1 = coupling[0] * inverse[0][1] + coupling[1] * inverse[1][1]
    rotated = rotation_ref[...] - map_0 * refusal_ref[0:1, :] - map_1 * refusal_ref[1:2, :]
    rows[...] = jnp.zeros_like(rows)
    rows[0:4, :] = rotated
    rows[4:6, :] = refusal_ref[...]
    along = summed[8:10, :npos]
    rank = lax.broadcasted_iota(jnp.int32, (4, npos), 0)
    bias = jnp.zeros((4, npos), f32)
    for r in range(4):
        bias = jnp.where(rank == r, bias_ref[r], bias)
    code = (
        summed[0:4, :npos]
        + bias
        - (summed[4:8, :npos] - map_0 * along[0:1, :] - map_1 * along[1:2, :])
    )
    spread = contract(select, code, 1, 1, highest)
    loads[9].wait()

    def later_forward(h, carry):
        @pl.when(z < last)
        def _():
            later_copy(h).wait_recv()

        @pl.when(jnp.logical_and(z > 0, z < last))
        def _():
            later[h] = later[h] + jnp.exp(group * log_decay(h)) * later_in[h]
            later_copy(h).start()

        return carry

    def state_forward(h, carry):
        @pl.when(z > 0)
        def _():
            state_copy(h).wait_recv()

        @pl.when(jnp.logical_and(z > 0, z < last))
        def _():
            state[h] = state[h] + jnp.exp(group * log_decay(h)) * state_in[h]
            state_copy(h).start()

        return carry

    def own_state(h):
        at = slice(h * size, (h + 1) * size)
        value = v_ref[0, :, at].astype(f32)
        shift = spread[:, 0:1] * rows[0:1, at]
        for r in range(1, 4):
            shift = shift + spread[:, r : r + 1] * rows[r : r + 1, at]
        value = (value + shift).astype(bf16)
        moved[:, at] = value
        weighted = value.astype(f32) * jnp.exp((group - 1.0 - offsets) * log_decay(h))
        both = jnp.concatenate(split(weighted), axis=1)
        state[h] = halves(contract(k_ref[0, :, at], both, 0, 0))

    own_state(0)

    @pl.when(z == 0)
    def _():
        state_copy(0).start()

    for h in range(1, heads):
        own_state(h)

    @pl.when(z == 0)
    def _():
        for h in range(1, heads):
            state_copy(h).start()

    def local(h):
        at = slice(h * size, (h + 1) * size)
        table = jnp.where(between >= 0, jnp.exp(apart * log_decay(h)), 0.0)
        query, key = q_ref[0, :, at], k_ref[0, :, at]
        grad, value = g_ref[0, :, at], moved[:, at]
        mixing = (contract(query, key, 1, 1) * table).astype(bf16)
        mixed = (contract(grad, value, 1, 1) * table).astype(bf16)
        grad_moved[:, at] = contract(mixing, grad, 0, 0)
        inner_key[:, at] = contract(mixed, query, 0, 0)
        inner[:, at] = contract(mixing, value, 1, 0)
        inner_query[:, at] = contract(mixed, key, 1, 0)

    near = z == last - 1
    half = heads // 2
    one = jnp.where(near, min(1, heads), 0)
    two = jnp.where(near, min(2, heads), 0)
    ahead = jnp.where(near, min(3, heads), jnp.where(z == last - 2, min(1, heads), 0))
    state_ahead = jnp.where(jnp.logical_and(z == 1, z < last), min(1, heads), 0)
    lax.fori_loop(0, one, later_forward, 0)
    for h in range(half):
        local(h)
    lax.fori_loop(one, two, later_forward, 0)
    for h in range(half, heads):
        local(h)
    lax.fori_loop(two, ahead, later_forward, 0)
    lax.fori_loop(0, state_ahead, state_forward, 0)

    def later_outer(h):
        at = pl.ds(pl.multiple_of(h * size, size), size)
        high, low = split(later_in[h])
        leave = jnp.exp((group - offsets) * log_decay(h))
        wide = grad_moved[:, at] + leave * halves(
            contract(k_ref[0, :, at], jnp.concatenate([high, low], axis=1), 1, 0)
        )
        grad_moved[:, at] = wide
        picks[:npos, at] = halves(
            contract(select_rows[...], jnp.concatenate(split(wide), axis=1), 1, 0)
        )
        grad_key = inner_key[:, at] + leave * halves(
            contract(moved[:, at], jnp.concatenate([high, low], axis=0), 1, 1)
        )
        grad_key_ref[0, :, at] = grad_key.astype(bf16)

    def state_outer(h):
        at = pl.ds(pl.multiple_of(h * size, size), size)
        high, low = split(state_in[h])
        enter = jnp.exp((offsets + 1.0) * log_decay(h))
        attended = inner[:, at] + enter * halves(
            contract(q_ref[0, :, at], jnp.concatenate([high, low], axis=1), 1, 0)
        )
        attended_ref[0, :, at] = attended.astype(bf16)
        grad_query = inner_query[:, at] + enter * halves(
            contract(g_ref[0, :, at], jnp.concatenate([high, low], axis=0), 1, 1)
        )
        grad_query_ref[0, :, at] = grad_query.astype(bf16)

    @pl.when(z == last)
    def _():
        for h in range(heads):
            later_outer(h)

    @pl.when(z < last)
    def _():
        def both_steps(i, carry):
            @pl.when(i + ahead < heads)
            def _():
                later_forward(jnp.minimum(i + ahead, heads - 1), 0)

            @pl.when(i + state_ahead < heads)
            def _():
                state_forward(jnp.minimum(i + state_ahead, heads - 1), 0)

            later_outer(i)
            state_outer(i)
            return carry

        lax.fori_loop(0, heads, both_steps, 0)

    stores[2].start()

    second[y] = jnp.zeros(second.shape[1:], f32)
    second[y, :, :npos] = contract(rows[...], picks[:npos, :], 1, 1, highest)
    for step in range(1, peers):
        across(second, second_send, second_recv, step).start()

    def part_copy(owner):
        target = owner * stride
        return pltpu.make_async_remote_copy(
            src_ref=pay.at[owner],
            dst_ref=parts.at[member],
            send_sem=parts_send.at[owner],
            recv_sem=parts_recv.at[member],
            device_id={"seq": target // docs, "dp": target % docs},
            device_id_type=MESH,
        )

    def finish_code():
        for step in range(1, peers):
            arrived(second, second_send, second_recv, step)
        sums = second[0]
        for peer in range(1, peers):
            sums = sums + second[peer]
        code_grad = sums[0:4, :npos]
        ahead = sums[4:6, :npos]
        projected = [
            jnp.sum(
                code * ahead[b : b + 1, :] - code_grad * along_own[b : b + 1, :],
                axis=1,
                keepdims=True,
            )
            for b in range(2)
        ]
        back_0 = projected[0] * inverse[0][0] + projected[1] * inverse[1][0]
        back_1 = projected[0] * inverse[0][1] + projected[1] * inverse[1][1]
        weight_part = contract(code_grad, stack[:npos, :], 1, 0, highest)
        rotation_part = (
            contract(code, picks[:npos, :], 1, 0, highest)
            - weight_part
            - back_0 * refusal_ref[0:1, :]
            - back_1 * refusal_ref[1:2, :]
        )
        bias_part = contract(jnp.ones((8, npos), f32), code_grad, 1, 1, highest)
        width = pay.shape[2]
        for owner in range(owners):
            at = slice(owner * width, (owner + 1) * width)
            pay[owner, 0:4, :] = rotation_part[:, at]
            pay[owner, 4:8, :] = weight_part[:, at]
            pay[owner, 8:16, :] = jnp.zeros((8, width), f32)
            pay[owner, 8:16, 0:4] = bias_part

            @pl.when(member == owner * stride)
            def _():
                parts[member] = pay[owner]

            @pl.when(member != owner * stride)
            def _():
                part_copy(owner).start()

        spread_grad = contract(select, code_grad, 1, 1, highest)
        for h in range(heads):
            at = slice(h * size, (h + 1) * size)
            wide = grad_moved[:, at]
            for r in range(4):
                wide = wide + spread_grad[:, r : r + 1] * (
                    weight_ref[r : r + 1, at] - rows[r : r + 1, at]
                )
            grad_value_ref[0, :, at] = wide.astype(bf16)
        stores[3].start()

    along_own = along

    @pl.when(z == last)
    def _():
        finish_code()

    @pl.when(z == last)
    def _():
        def rest(i, carry):
            state_forward(i, 0)
            state_outer(i)
            return carry

        lax.fori_loop(0, heads, rest, 0)

    stores[0].start()
    stores[1].start()

    @pl.when(z < last)
    def _():
        finish_code()

    mine = member // stride
    owning = lax.rem(member, stride) == 0

    def total_copy(step):
        other = lax.rem(member + step, members)
        return pltpu.make_async_remote_copy(
            src_ref=total.at[mine],
            dst_ref=total.at[mine],
            send_sem=total_send.at[step],
            recv_sem=total_recv.at[mine],
            device_id={"seq": other // docs, "dp": lax.rem(other, docs)},
            device_id_type=MESH,
        )

    def part_arrived(step, carry):
        other = lax.rem(member + step, members)
        pltpu.make_async_remote_copy(
            src_ref=pay.at[0],
            dst_ref=parts.at[other],
            send_sem=parts_send.at[0],
            recv_sem=parts_recv.at[other],
            device_id={"seq": other // docs, "dp": lax.rem(other, docs)},
            device_id_type=MESH,
        ).wait_recv()
        return carry

    def total_start(step, carry):
        total_copy(step).start()
        return carry

    def total_sent(step, carry):
        total_copy(step).wait_send()
        return carry

    @pl.when(owning)
    def _():
        lax.fori_loop(1, members, part_arrived, 0)
        total[mine] = jnp.sum(parts[...], axis=0)
        lax.fori_loop(1, members, total_start, 0)

    width = pay.shape[2]
    for owner in range(owners):

        @pl.when(member != owner * stride)
        def _():
            pltpu.make_async_remote_copy(
                src_ref=total.at[owner],
                dst_ref=total.at[owner],
                send_sem=total_send.at[0],
                recv_sem=total_recv.at[owner],
                device_id={"seq": (owner * stride) // docs, "dp": (owner * stride) % docs},
                device_id_type=MESH,
            ).wait_recv()

    for owner in range(owners):
        at = slice(owner * width, (owner + 1) * width)
        grad_rotation_ref[:, at] = total[owner, 0:4, :]
        grad_weight_ref[:, at] = total[owner, 4:8, :]
    grad_bias_ref[...] = total[0, 8:9, 0:4]
    for i in range(4, 7):
        stores[i].start()

    for i in range(7):
        stores[i].wait()
    for step in range(1, peers):
        across(first, first_send, first_recv, step).wait_send()
        across(second, second_send, second_recv, step).wait_send()

    def sent(h, carry):
        @pl.when(z < last)
        def _():
            state_copy(h).wait_send()

        @pl.when(z > 0)
        def _():
            later_copy(h).wait_send()

        return carry

    lax.fori_loop(0, heads, sent, 0)
    for owner in range(owners):

        @pl.when(member != owner * stride)
        def _():
            part_copy(owner).wait_send()

    @pl.when(owning)
    def _():
        lax.fori_loop(1, members, total_sent, 0)


def store(*refs):
    sources, targets, held, sems = refs[:7], refs[7:14], refs[14:21], refs[21]
    fetches = [pltpu.make_async_copy(sources[i], held[i], sems.at[0, i]) for i in range(7)]
    copies = [pltpu.make_async_copy(held[i], targets[i], sems.at[1, i]) for i in range(7)]
    for fetch in fetches:
        fetch.start()
    for fetch, copy in zip(fetches, copies):
        fetch.wait()
        copy.start()
    for copy in copies:
        copy.wait()


def shards(mesh, *arrays):
    (queries, key_rows, values, out_grad, decay_rate, rotation, refusal, weight, bias, positions) = (
        arrays
    )
    seqs, peers, docs = mesh.shape["seq"], mesh.shape["head"], mesh.shape["dp"]
    heads = decay_rate.shape[0]
    group, width = queries.shape[1], queries.shape[2]
    size = width // heads
    npos = positions.shape[1]
    members = seqs * docs
    owners = min(members, width // 128)
    limit = 60 * 1024 * 1024
    hbm = pl.BlockSpec(memory_space=pltpu.HBM)
    dma = pltpu.SemaphoreType.DMA
    square = (heads, size, size)
    big = jax.ShapeDtypeStruct(queries.shape, bf16)
    results = pl.pallas_call(
        functools.partial(kernel, (seqs, peers, docs, heads, owners)),
        out_shape=(
            big,
            big,
            big,
            big,
            jax.ShapeDtypeStruct(rotation.shape, f32),
            jax.ShapeDtypeStruct(weight.shape, f32),
            jax.ShapeDtypeStruct((1,) + bias.shape, f32),
        ),
        in_specs=[hbm] * 10,
        out_specs=(hbm,) * 7,
        scratch_shapes=[
            pltpu.VMEM(queries.shape, bf16),
            pltpu.VMEM(queries.shape, bf16),
            pltpu.VMEM(queries.shape, bf16),
            pltpu.VMEM(queries.shape, bf16),
            pltpu.VMEM(rotation.shape, f32),
            pltpu.VMEM(weight.shape, f32),
            pltpu.VMEM((1,) + bias.shape, f32),
            dma((7,)),
            pltpu.VMEM(queries.shape, bf16),
            pltpu.VMEM(queries.shape, bf16),
            pltpu.VMEM(queries.shape, bf16),
            pltpu.VMEM(queries.shape, bf16),
            pltpu.SMEM(decay_rate.shape, f32),
            pltpu.VMEM(rotation.shape, f32),
            pltpu.VMEM((2, width), f32),
            pltpu.VMEM(weight.shape, f32),
            pltpu.SMEM(bias.shape, f32),
            pltpu.VMEM(positions.shape, jnp.int32),
            dma((10,)),
            pltpu.VMEM((npos, group), bf16),
            pltpu.VMEM((group, width), f32),
            pltpu.VMEM((group, width), f32),
            pltpu.VMEM((group, width), f32),
            pltpu.VMEM((npos + 16, width), f32),
            pltpu.VMEM((npos, width), f32),
            pltpu.VMEM((8, width), f32),
            pltpu.VMEM((group, width), bf16),
            pltpu.VMEM((group, width), f32),
            pltpu.VMEM(square, f32),
            pltpu.VMEM(square, f32),
            pltpu.VMEM(square, f32),
            pltpu.VMEM(square, f32),
            pltpu.VMEM((peers, 16, 128), f32),
            pltpu.VMEM((peers, 8, 128), f32),
            pltpu.VMEM((owners, 16, width // owners), f32),
            pltpu.VMEM((members, 16, width // owners), f32),
            pltpu.VMEM((owners, 16, width // owners), f32),
            dma((peers,)),
            dma((peers,)),
            dma((peers,)),
            dma((peers,)),
            dma((heads,)),
            dma((heads,)),
            dma((heads,)),
            dma((heads,)),
            dma((owners,)),
            dma((members,)),
            dma((members,)),
            dma((owners,)),
        ],
        compiler_params=pltpu.CompilerParams(
            collective_id=0, has_side_effects=True, vmem_limit_bytes=limit
        ),
    )(queries, key_rows, values, out_grad, decay_rate, rotation, refusal.T, weight, bias, positions)
    results = pl.pallas_call(
        store,
        out_shape=tuple(jax.ShapeDtypeStruct(x.shape, x.dtype) for x in results),
        in_specs=[hbm] * 7,
        out_specs=(hbm,) * 7,
        scratch_shapes=[pltpu.VMEM(x.shape, x.dtype) for x in results] + [dma((2, 7))],
        compiler_params=pltpu.CompilerParams(vmem_limit_bytes=limit),
    )(*results)
    return results[:6] + (results[6].reshape(bias.shape),)


def solution(mesh):
    return jax.shard_map(
        functools.partial(shards, mesh),
        mesh=mesh,
        in_specs=(
            P("dp", "seq", "head"),
            P("dp", "seq", "head"),
            P("dp", "seq", "head"),
            P("dp", "seq", "head"),
            P("head"),
            P(None, "head"),
            P("head", None),
            P(None, "head"),
            P(),
            P("dp", None),
        ),
        out_specs=(
            P("dp", "seq", "head"),
            P("dp", "seq", "head"),
            P("dp", "seq", "head"),
            P("dp", "seq", "head"),
            P(None, "head"),
            P(None, "head"),
            P(),
        ),
        check_vma=False,
    )
```

```python
import functools
import jax
import jax.numpy as jnp
from jax import lax
from jax.experimental import pallas as pl
from jax.experimental.pallas import tpu as pltpu
from jax.sharding import PartitionSpec as P

highest = lax.Precision.HIGHEST
MESH = pl.DeviceIdType.MESH
f32 = jnp.float32
bf16 = jnp.bfloat16
PIECES = 4


def contract(a, b, da, db, precision=None):
    return lax.dot_general(
        a, b, (((da,), (db,)), ((), ())), precision=precision, preferred_element_type=f32
    )


def split(x):
    high = x.astype(bf16)
    return high, (x - high.astype(f32)).astype(bf16)


def halves(x):
    n = x.shape[1] // 2
    return x[:, :n] + x[:, n:]


def kernel(
    sizes,
    q_in,
    k_in,
    v_in,
    g_in,
    decay_in,
    rotation_in,
    refusal_in,
    weight_in,
    bias_in,
    positions_in,
    attended_out,
    grad_query_out,
    grad_key_out,
    grad_value_out,
    grad_rotation_out,
    grad_weight_out,
    grad_bias_out,
    attended_ref,
    grad_query_ref,
    grad_key_ref,
    grad_value_ref,
    grad_rotation_ref,
    grad_weight_ref,
    grad_bias_ref,
    store_sem,
    q_ref,
    k_ref,
    v_ref,
    g_ref,
    decay_ref,
    rotation_ref,
    refusal_ref,
    weight_ref,
    bias_ref,
    positions_ref,
    load_sem,
    select_rows,
    inner,
    inner_query,
    inner_key,
    stack,
    picks,
    rows,
    moved,
    grad_moved,
    state,
    state_in,
    later,
    later_in,
    first,
    second,
    pay,
    parts,
    total,
    first_send,
    first_recv,
    second_send,
    second_recv,
    state_send,
    state_recv,
    later_send,
    later_recv,
    parts_send,
    parts_recv,
    total_send,
    total_recv,
):
    seqs, peers, docs, heads, owners = sizes
    group = q_ref.shape[1]
    size = q_ref.shape[2] // heads
    npos = positions_ref.shape[1]
    members = seqs * docs
    stride = members // owners
    z, y, c = lax.axis_index("seq"), lax.axis_index("head"), lax.axis_index("dp")
    last = seqs - 1
    member = z * docs + c

    loads = [
        pltpu.make_async_copy(source, target, load_sem.at[i])
        for i, (source, target) in enumerate(
            (
                (v_in, v_ref),
                (positions_in, positions_ref),
                (weight_in, weight_ref),
                (rotation_in, rotation_ref),
                (refusal_in, refusal_ref),
                (q_in, q_ref),
                (g_in, g_ref),
                (decay_in, decay_ref),
                (bias_in, bias_ref),
                (k_in, k_ref),
            )
        )
    ]
    for load in loads:
        load.start()
    stores = [
        pltpu.make_async_copy(source, target, store_sem.at[i])
        for i, (source, target) in enumerate(
            (
                (attended_ref, attended_out),
                (grad_query_ref, grad_query_out),
                (grad_key_ref, grad_key_out),
                (grad_value_ref, grad_value_out),
                (grad_rotation_ref, grad_rotation_out),
                (grad_weight_ref, grad_weight_out),
                (grad_bias_ref, grad_bias_out),
            )
        )
    ]
    barrier = pltpu.get_barrier_semaphore()
    for step in range(1, peers):
        pl.semaphore_signal(
            barrier, inc=1, device_id={"head": lax.rem(y + step, peers)}, device_id_type=MESH
        )

    def greet(step, carry):
        other = lax.rem(member + step, members)
        pl.semaphore_signal(
            barrier,
            inc=1,
            device_id={"seq": other // docs, "dp": lax.rem(other, docs)},
            device_id_type=MESH,
        )
        return carry

    lax.fori_loop(1, members, greet, 0)

    def across(buffer, send, recv, step):
        other = lax.rem(y + step, peers)
        return pltpu.make_async_remote_copy(
            src_ref=buffer.at[y],
            dst_ref=buffer.at[y],
            send_sem=send.at[step - 1],
            recv_sem=recv.at[y],
            device_id={"head": other},
            device_id_type=MESH,
        )

    def arrived(buffer, send, recv, step):
        other = lax.rem(y + step, peers)
        pltpu.make_async_remote_copy(
            src_ref=buffer.at[other],
            dst_ref=buffer.at[other],
            send_sem=send.at[step - 1],
            recv_sem=recv.at[other],
            device_id={"head": other},
            device_id_type=MESH,
        ).wait_recv()

    depth = size // PIECES
    pieces = heads * PIECES

    def piece(n):
        if isinstance(n, int):
            return n // PIECES, slice(n % PIECES * depth, (n % PIECES + 1) * depth)
        return n // PIECES, pl.ds(pl.multiple_of(lax.rem(n, PIECES) * depth, depth), depth)

    def state_copy(n):
        h, at = piece(n)
        return pltpu.make_async_remote_copy(
            src_ref=state.at[h, at],
            dst_ref=state_in.at[h, at],
            send_sem=state_send.at[n],
            recv_sem=state_recv.at[n],
            device_id={"seq": lax.rem(z + 1, seqs)},
            device_id_type=MESH,
        )

    def later_copy(n):
        h, at = piece(n)
        return pltpu.make_async_remote_copy(
            src_ref=later.at[h, at],
            dst_ref=later_in.at[h, at],
            send_sem=later_send.at[n],
            recv_sem=later_recv.at[n],
            device_id={"seq": lax.rem(z + seqs - 1, seqs)},
            device_id_type=MESH,
        )

    offsets = lax.broadcasted_iota(jnp.int32, (group, size), 0).astype(f32)

    def log_decay(h):
        return jnp.log1p(-jnp.full((1, size), decay_ref[h], f32))

    for load in loads[:5]:
        load.wait()
    places = z * group + lax.broadcasted_iota(jnp.int32, (group, npos), 0)
    chosen = places == positions_ref[...]
    select = jnp.where(chosen, 1.0, 0.0)
    turned = select.T
    select_rows[...] = turned.astype(bf16)
    stack[npos:, :] = jnp.zeros((stack.shape[0] - npos, stack.shape[1]), f32)
    picked = contract(select_rows[...], v_ref[0], 1, 0)
    stack[:npos, :] = picked
    stack[npos : npos + 4, :] = weight_ref[...]
    stack[npos + 4 : npos + 8, :] = rotation_ref[...]
    stack[npos + 8 : npos + 10, :] = refusal_ref[...]
    first[y] = jnp.zeros(first.shape[1:], f32)
    first[y, :, : stack.shape[0]] = contract(stack[npos:, :], stack[...], 1, 1, highest)
    pl.semaphore_wait(barrier, peers - 1 + members - 1)
    for step in range(1, peers):
        across(first, first_send, first_recv, step).start()

    for load in loads[5:8]:
        load.wait()

    def own_later(h):
        at = slice(h * size, (h + 1) * size)
        weighted = g_ref[0, :, at].astype(f32) * jnp.exp(offsets * log_decay(h))
        both = jnp.concatenate(split(weighted), axis=1)
        later[h] = halves(contract(q_ref[0, :, at], both, 0, 0))

    own_later(0)

    @pl.when(z == last)
    def _():
        for n in range(PIECES):
            later_copy(n).start()

    for h in range(1, heads):
        own_later(h)

    @pl.when(z == last)
    def _():
        for n in range(PIECES, pieces):
            later_copy(n).start()

    @pl.when(z == last)
    def _():
        later_in[...] = jnp.zeros_like(later_in)

    @pl.when(z == 0)
    def _():
        state_in[...] = jnp.zeros_like(state_in)

    between = lax.broadcasted_iota(jnp.int32, (group, group), 0) - lax.broadcasted_iota(
        jnp.int32, (group, group), 1
    )
    apart = jnp.maximum(between, 0).astype(f32)

    loads[8].wait()
    for step in range(1, peers):
        arrived(first, first_send, first_recv, step)
    summed = first[0]
    for peer in range(1, peers):
        summed = summed + first[peer]
    at_ref = npos + 8
    gram = [
        [summed[8 + a : 9 + a, at_ref + b : at_ref + b + 1] for b in range(2)] for a in range(2)
    ]
    determinant = gram[0][0] * gram[1][1] - gram[0][1] * gram[1][0]
    inverse = [
        [gram[1][1] / determinant, -gram[0][1] / determinant],
        [-gram[1][0] / determinant, gram[0][0] / determinant],
    ]
    coupling = [summed[4:8, at_ref + b : at_ref + b + 1] for b in range(2)]
    map_0 = coupling[0] * inverse[0][0] + coupling[1] * inverse[1][0]
    map_1 = coupling[0] * inverse[0][1] + coupling[1] * inverse[1][1]
    rotated = rotation_ref[...] - map_0 * refusal_ref[0:1, :] - map_1 * refusal_ref[1:2, :]
    rows[...] = jnp.zeros_like(rows)
    rows[0:4, :] = rotated
    rows[4:6, :] = refusal_ref[...]
    along = summed[8:10, :npos]
    rank = lax.broadcasted_iota(jnp.int32, (4, npos), 0)
    bias = jnp.zeros((4, npos), f32)
    for r in range(4):
        bias = jnp.where(rank == r, bias_ref[r], bias)
    code = (
        summed[0:4, :npos]
        + bias
        - (summed[4:8, :npos] - map_0 * along[0:1, :] - map_1 * along[1:2, :])
    )
    spread = contract(select, code, 1, 1, highest)
    loads[9].wait()

    def later_forward(n, carry):
        h, at = piece(n)

        @pl.when(z < last)
        def _():
            later_copy(n).wait_recv()

        @pl.when(jnp.logical_and(z > 0, z < last))
        def _():
            later[h, at] = later[h, at] + jnp.exp(group * log_decay(h)) * later_in[h, at]
            later_copy(n).start()

        return carry

    def state_forward(n, carry):
        h, at = piece(n)

        @pl.when(z > 0)
        def _():
            state_copy(n).wait_recv()

        @pl.when(jnp.logical_and(z > 0, z < last))
        def _():
            state[h, at] = state[h, at] + jnp.exp(group * log_decay(h)) * state_in[h, at]
            state_copy(n).start()

        return carry

    def own_state(h):
        at = slice(h * size, (h + 1) * size)
        value = v_ref[0, :, at].astype(f32)
        shift = spread[:, 0:1] * rows[0:1, at]
        for r in range(1, 4):
            shift = shift + spread[:, r : r + 1] * rows[r : r + 1, at]
        value = (value + shift).astype(bf16)
        moved[:, at] = value
        weighted = value.astype(f32) * jnp.exp((group - 1.0 - offsets) * log_decay(h))
        both = jnp.concatenate(split(weighted), axis=1)
        state[h] = halves(contract(k_ref[0, :, at], both, 0, 0))

    own_state(0)

    @pl.when(z == 0)
    def _():
        for n in range(PIECES):
            state_copy(n).start()

    for h in range(1, heads):
        own_state(h)

    @pl.when(z == 0)
    def _():
        for n in range(PIECES, pieces):
            state_copy(n).start()

    def local(h):
        at = slice(h * size, (h + 1) * size)
        table = jnp.where(between >= 0, jnp.exp(apart * log_decay(h)), 0.0)
        query, key = q_ref[0, :, at], k_ref[0, :, at]
        grad, value = g_ref[0, :, at], moved[:, at]
        mixing = (contract(query, key, 1, 1) * table).astype(bf16)
        mixed = (contract(grad, value, 1, 1) * table).astype(bf16)
        grad_moved[:, at] = contract(mixing, grad, 0, 0)
        inner_key[:, at] = contract(mixed, query, 0, 0)
        inner[:, at] = contract(mixing, value, 1, 0)
        inner_query[:, at] = contract(mixed, key, 1, 0)

    near = z == last - 1
    far = jnp.logical_and(z == 1, z < last - 1)
    blocks = 4
    later_plan = (3, 4, 5, 6, 6)
    state_plan = (0, 0, 1, 2, 2)
    laters, states = 0, 0
    for block in range(blocks + 1):
        for h in range((block - 1) * heads // blocks, block * heads // blocks):
            if block > 0:
                local(h)
        goal = jnp.where(near, min(later_plan[block], pieces), 0)
        lax.fori_loop(laters, goal, later_forward, 0)
        laters = goal
        goal = jnp.where(far, min(state_plan[block], pieces), 0)
        lax.fori_loop(states, goal, state_forward, 0)
        states = goal

    def later_outer(h):
        at = pl.ds(pl.multiple_of(h * size, size), size)
        high, low = split(later_in[h])
        leave = jnp.exp((group - offsets) * log_decay(h))
        wide = grad_moved[:, at] + leave * halves(
            contract(k_ref[0, :, at], jnp.concatenate([high, low], axis=1), 1, 0)
        )
        grad_moved[:, at] = wide
        picks[:npos, at] = halves(
            contract(select_rows[...], jnp.concatenate(split(wide), axis=1), 1, 0)
        )
        grad_key = inner_key[:, at] + leave * halves(
            contract(moved[:, at], jnp.concatenate([high, low], axis=0), 1, 1)
        )
        grad_key_ref[0, :, at] = grad_key.astype(bf16)

    def state_outer(h):
        at = pl.ds(pl.multiple_of(h * size, size), size)
        high, low = split(state_in[h])
        enter = jnp.exp((offsets + 1.0) * log_decay(h))
        attended = inner[:, at] + enter * halves(
            contract(q_ref[0, :, at], jnp.concatenate([high, low], axis=1), 1, 0)
        )
        attended_ref[0, :, at] = attended.astype(bf16)
        grad_query = inner_query[:, at] + enter * halves(
            contract(g_ref[0, :, at], jnp.concatenate([high, low], axis=0), 1, 1)
        )
        grad_query_ref[0, :, at] = grad_query.astype(bf16)

    @pl.when(z == last)
    def _():
        for h in range(heads):
            later_outer(h)

    @pl.when(z < last)
    def _():
        def both_steps(n, carry):
            @pl.when(n + laters < pieces)
            def _():
                later_forward(jnp.minimum(n + laters, pieces - 1), 0)

            @pl.when(n + states < pieces)
            def _():
                state_forward(jnp.minimum(n + states, pieces - 1), 0)

            @pl.when(lax.rem(n, PIECES) == PIECES - 1)
            def _():
                later_outer(n // PIECES)
                state_outer(n // PIECES)

            return carry

        lax.fori_loop(0, pieces, both_steps, 0)

    stores[2].start()

    second[y] = jnp.zeros(second.shape[1:], f32)
    second[y, :, :npos] = contract(rows[...], picks[:npos, :], 1, 1, highest)
    for step in range(1, peers):
        across(second, second_send, second_recv, step).start()

    def part_copy(owner):
        target = owner * stride
        return pltpu.make_async_remote_copy(
            src_ref=pay.at[owner],
            dst_ref=parts.at[member],
            send_sem=parts_send.at[owner],
            recv_sem=parts_recv.at[member],
            device_id={"seq": target // docs, "dp": target % docs},
            device_id_type=MESH,
        )

    def finish_code():
        for step in range(1, peers):
            arrived(second, second_send, second_recv, step)
        sums = second[0]
        for peer in range(1, peers):
            sums = sums + second[peer]
        code_grad = sums[0:4, :npos]
        ahead = sums[4:6, :npos]
        projected = [
            jnp.sum(
                code * ahead[b : b + 1, :] - code_grad * along_own[b : b + 1, :],
                axis=1,
                keepdims=True,
            )
            for b in range(2)
        ]
        back_0 = projected[0] * inverse[0][0] + projected[1] * inverse[1][0]
        back_1 = projected[0] * inverse[0][1] + projected[1] * inverse[1][1]
        weight_part = contract(code_grad, stack[:npos, :], 1, 0, highest)
        rotation_part = (
            contract(code, picks[:npos, :], 1, 0, highest)
            - weight_part
            - back_0 * refusal_ref[0:1, :]
            - back_1 * refusal_ref[1:2, :]
        )
        bias_part = contract(jnp.ones((8, npos), f32), code_grad, 1, 1, highest)
        width = pay.shape[2]
        for owner in range(owners):
            at = slice(owner * width, (owner + 1) * width)
            pay[owner, 0:4, :] = rotation_part[:, at]
            pay[owner, 4:8, :] = weight_part[:, at]
            pay[owner, 8:16, :] = jnp.zeros((8, width), f32)
            pay[owner, 8:16, 0:4] = bias_part

            @pl.when(member == owner * stride)
            def _():
                parts[member] = pay[owner]

            @pl.when(member != owner * stride)
            def _():
                part_copy(owner).start()

        spread_grad = contract(select, code_grad, 1, 1, highest)
        for h in range(heads):
            at = slice(h * size, (h + 1) * size)
            wide = grad_moved[:, at]
            for r in range(4):
                wide = wide + spread_grad[:, r : r + 1] * (
                    weight_ref[r : r + 1, at] - rows[r : r + 1, at]
                )
            grad_value_ref[0, :, at] = wide.astype(bf16)
        stores[3].start()

    along_own = along

    @pl.when(z == last)
    def _():
        finish_code()

    @pl.when(z == last)
    def _():
        def rest(i, carry):
            for p in range(PIECES):
                state_forward(i * PIECES + p, 0)
            state_outer(i)
            return carry

        lax.fori_loop(0, heads, rest, 0)

    stores[0].start()
    stores[1].start()

    @pl.when(z < last)
    def _():
        finish_code()

    mine = member // stride
    owning = lax.rem(member, stride) == 0

    def total_copy(step):
        other = lax.rem(member + step, members)
        return pltpu.make_async_remote_copy(
            src_ref=total.at[mine],
            dst_ref=total.at[mine],
            send_sem=total_send.at[step],
            recv_sem=total_recv.at[mine],
            device_id={"seq": other // docs, "dp": lax.rem(other, docs)},
            device_id_type=MESH,
        )

    def part_arrived(step, carry):
        other = lax.rem(member + step, members)
        pltpu.make_async_remote_copy(
            src_ref=pay.at[0],
            dst_ref=parts.at[other],
            send_sem=parts_send.at[0],
            recv_sem=parts_recv.at[other],
            device_id={"seq": other // docs, "dp": lax.rem(other, docs)},
            device_id_type=MESH,
        ).wait_recv()
        return carry

    def total_start(step, carry):
        total_copy(step).start()
        return carry

    def total_sent(step, carry):
        total_copy(step).wait_send()
        return carry

    @pl.when(owning)
    def _():
        lax.fori_loop(1, members, part_arrived, 0)
        total[mine] = jnp.sum(parts[...], axis=0)
        lax.fori_loop(1, members, total_start, 0)

    width = pay.shape[2]
    for owner in range(owners):

        @pl.when(member != owner * stride)
        def _():
            pltpu.make_async_remote_copy(
                src_ref=total.at[owner],
                dst_ref=total.at[owner],
                send_sem=total_send.at[0],
                recv_sem=total_recv.at[owner],
                device_id={"seq": (owner * stride) // docs, "dp": (owner * stride) % docs},
                device_id_type=MESH,
            ).wait_recv()

    for owner in range(owners):
        at = slice(owner * width, (owner + 1) * width)
        grad_rotation_ref[:, at] = total[owner, 0:4, :]
        grad_weight_ref[:, at] = total[owner, 4:8, :]
    grad_bias_ref[...] = total[0, 8:9, 0:4]
    for i in range(4, 7):
        stores[i].start()

    for i in range(7):
        stores[i].wait()
    for step in range(1, peers):
        across(first, first_send, first_recv, step).wait_send()
        across(second, second_send, second_recv, step).wait_send()

    def sent(n, carry):
        @pl.when(z < last)
        def _():
            state_copy(n).wait_send()

        @pl.when(z > 0)
        def _():
            later_copy(n).wait_send()

        return carry

    lax.fori_loop(0, pieces, sent, 0)
    for owner in range(owners):

        @pl.when(member != owner * stride)
        def _():
            part_copy(owner).wait_send()

    @pl.when(owning)
    def _():
        lax.fori_loop(1, members, total_sent, 0)


def store(*refs):
    sources, targets, held, sems = refs[:7], refs[7:14], refs[14:21], refs[21]
    fetches = [pltpu.make_async_copy(sources[i], held[i], sems.at[0, i]) for i in range(7)]
    copies = [pltpu.make_async_copy(held[i], targets[i], sems.at[1, i]) for i in range(7)]
    for fetch in fetches:
        fetch.start()
    for fetch, copy in zip(fetches, copies):
        fetch.wait()
        copy.start()
    for copy in copies:
        copy.wait()


def shards(mesh, *arrays):
    (queries, key_rows, values, out_grad, decay_rate, rotation, refusal, weight, bias, positions) = (
        arrays
    )
    seqs, peers, docs = mesh.shape["seq"], mesh.shape["head"], mesh.shape["dp"]
    heads = decay_rate.shape[0]
    group, width = queries.shape[1], queries.shape[2]
    size = width // heads
    npos = positions.shape[1]
    members = seqs * docs
    owners = min(members, width // 128)
    limit = 60 * 1024 * 1024
    hbm = pl.BlockSpec(memory_space=pltpu.HBM)
    dma = pltpu.SemaphoreType.DMA
    square = (heads, size, size)
    big = jax.ShapeDtypeStruct(queries.shape, bf16)
    results = pl.pallas_call(
        functools.partial(kernel, (seqs, peers, docs, heads, owners)),
        out_shape=(
            big,
            big,
            big,
            big,
            jax.ShapeDtypeStruct(rotation.shape, f32),
            jax.ShapeDtypeStruct(weight.shape, f32),
            jax.ShapeDtypeStruct((1,) + bias.shape, f32),
        ),
        in_specs=[hbm] * 10,
        out_specs=(hbm,) * 7,
        scratch_shapes=[
            pltpu.VMEM(queries.shape, bf16),
            pltpu.VMEM(queries.shape, bf16),
            pltpu.VMEM(queries.shape, bf16),
            pltpu.VMEM(queries.shape, bf16),
            pltpu.VMEM(rotation.shape, f32),
            pltpu.VMEM(weight.shape, f32),
            pltpu.VMEM((1,) + bias.shape, f32),
            dma((7,)),
            pltpu.VMEM(queries.shape, bf16),
            pltpu.VMEM(queries.shape, bf16),
            pltpu.VMEM(queries.shape, bf16),
            pltpu.VMEM(queries.shape, bf16),
            pltpu.SMEM(decay_rate.shape, f32),
            pltpu.VMEM(rotation.shape, f32),
            pltpu.VMEM((2, width), f32),
            pltpu.VMEM(weight.shape, f32),
            pltpu.SMEM(bias.shape, f32),
            pltpu.VMEM(positions.shape, jnp.int32),
            dma((10,)),
            pltpu.VMEM((npos, group), bf16),
            pltpu.VMEM((group, width), f32),
            pltpu.VMEM((group, width), f32),
            pltpu.VMEM((group, width), f32),
            pltpu.VMEM((npos + 16, width), f32),
            pltpu.VMEM((npos, width), f32),
            pltpu.VMEM((8, width), f32),
            pltpu.VMEM((group, width), bf16),
            pltpu.VMEM((group, width), f32),
            pltpu.VMEM(square, f32),
            pltpu.VMEM(square, f32),
            pltpu.VMEM(square, f32),
            pltpu.VMEM(square, f32),
            pltpu.VMEM((peers, 16, 128), f32),
            pltpu.VMEM((peers, 8, 128), f32),
            pltpu.VMEM((owners, 16, width // owners), f32),
            pltpu.VMEM((members, 16, width // owners), f32),
            pltpu.VMEM((owners, 16, width // owners), f32),
            dma((peers,)),
            dma((peers,)),
            dma((peers,)),
            dma((peers,)),
            dma((heads * PIECES,)),
            dma((heads * PIECES,)),
            dma((heads * PIECES,)),
            dma((heads * PIECES,)),
            dma((owners,)),
            dma((members,)),
            dma((members,)),
            dma((owners,)),
        ],
        compiler_params=pltpu.CompilerParams(
            collective_id=0, has_side_effects=True, vmem_limit_bytes=limit
        ),
    )(queries, key_rows, values, out_grad, decay_rate, rotation, refusal.T, weight, bias, positions)
    results = pl.pallas_call(
        store,
        out_shape=tuple(jax.ShapeDtypeStruct(x.shape, x.dtype) for x in results),
        in_specs=[hbm] * 7,
        out_specs=(hbm,) * 7,
        scratch_shapes=[pltpu.VMEM(x.shape, x.dtype) for x in results] + [dma((2, 7))],
        compiler_params=pltpu.CompilerParams(vmem_limit_bytes=limit),
    )(*results)
    return results[:6] + (results[6].reshape(bias.shape),)


def solution(mesh):
    return jax.shard_map(
        functools.partial(shards, mesh),
        mesh=mesh,
        in_specs=(
            P("dp", "seq", "head"),
            P("dp", "seq", "head"),
            P("dp", "seq", "head"),
            P("dp", "seq", "head"),
            P("head"),
            P(None, "head"),
            P("head", None),
            P(None, "head"),
            P(),
            P("dp", None),
        ),
        out_specs=(
            P("dp", "seq", "head"),
            P("dp", "seq", "head"),
            P("dp", "seq", "head"),
            P("dp", "seq", "head"),
            P(None, "head"),
            P(None, "head"),
            P(),
        ),
        check_vma=False,
    )
```

```python
import functools
import jax
import jax.numpy as jnp
from jax import lax
from jax.experimental import pallas as pl
from jax.experimental.pallas import tpu as pltpu
from jax.sharding import PartitionSpec as P

highest = lax.Precision.HIGHEST
MESH = pl.DeviceIdType.MESH
f32 = jnp.float32
bf16 = jnp.bfloat16


def contract(a, b, da, db, precision=None):
    return lax.dot_general(
        a, b, (((da,), (db,)), ((), ())), precision=precision, preferred_element_type=f32
    )


def split(x):
    high = x.astype(bf16)
    return high, (x - high.astype(f32)).astype(bf16)


def halves(x):
    n = x.shape[1] // 2
    return x[:, :n] + x[:, n:]


def kernel(
    sizes,
    q_in,
    k_in,
    v_in,
    g_in,
    decay_in,
    rotation_in,
    refusal_in,
    weight_in,
    bias_in,
    positions_in,
    attended_out,
    grad_query_out,
    grad_key_out,
    grad_value_out,
    grad_rotation_out,
    grad_weight_out,
    grad_bias_out,
    attended_ref,
    grad_query_ref,
    grad_key_ref,
    grad_value_ref,
    grad_rotation_ref,
    grad_weight_ref,
    grad_bias_ref,
    store_sem,
    q_ref,
    k_ref,
    v_ref,
    g_ref,
    decay_ref,
    rotation_ref,
    refusal_ref,
    weight_ref,
    bias_ref,
    positions_ref,
    load_sem,
    select_rows,
    inner,
    inner_query,
    inner_key,
    stack,
    picks,
    rows,
    moved,
    grad_moved,
    state,
    state_in,
    later,
    later_in,
    first,
    second,
    pay,
    parts,
    total,
    first_send,
    first_recv,
    second_send,
    second_recv,
    state_send,
    state_recv,
    later_send,
    later_recv,
    parts_send,
    parts_recv,
    total_send,
    total_recv,
):
    seqs, peers, docs, heads, owners = sizes
    group = q_ref.shape[1]
    size = q_ref.shape[2] // heads
    npos = positions_ref.shape[1]
    members = seqs * docs
    stride = members // owners
    z, y, c = lax.axis_index("seq"), lax.axis_index("head"), lax.axis_index("dp")
    last = seqs - 1
    member = z * docs + c

    loads = [
        pltpu.make_async_copy(source, target, load_sem.at[i])
        for i, (source, target) in enumerate(
            (
                (v_in, v_ref),
                (positions_in, positions_ref),
                (weight_in, weight_ref),
                (rotation_in, rotation_ref),
                (refusal_in, refusal_ref),
                (q_in, q_ref),
                (g_in, g_ref),
                (decay_in, decay_ref),
                (bias_in, bias_ref),
                (k_in, k_ref),
            )
        )
    ]
    for load in loads:
        load.start()
    stores = [
        pltpu.make_async_copy(source, target, store_sem.at[i])
        for i, (source, target) in enumerate(
            (
                (attended_ref, attended_out),
                (grad_query_ref, grad_query_out),
                (grad_key_ref, grad_key_out),
                (grad_value_ref, grad_value_out),
                (grad_rotation_ref, grad_rotation_out),
                (grad_weight_ref, grad_weight_out),
                (grad_bias_ref, grad_bias_out),
            )
        )
    ]
    barrier = pltpu.get_barrier_semaphore()
    for step in range(1, peers):
        pl.semaphore_signal(
            barrier, inc=1, device_id={"head": lax.rem(y + step, peers)}, device_id_type=MESH
        )

    def greet(step, carry):
        other = lax.rem(member + step, members)
        pl.semaphore_signal(
            barrier,
            inc=1,
            device_id={"seq": other // docs, "dp": lax.rem(other, docs)},
            device_id_type=MESH,
        )
        return carry

    lax.fori_loop(1, members, greet, 0)

    def across(buffer, send, recv, step):
        other = lax.rem(y + step, peers)
        return pltpu.make_async_remote_copy(
            src_ref=buffer.at[y],
            dst_ref=buffer.at[y],
            send_sem=send.at[step - 1],
            recv_sem=recv.at[y],
            device_id={"head": other},
            device_id_type=MESH,
        )

    def arrived(buffer, send, recv, step):
        other = lax.rem(y + step, peers)
        pltpu.make_async_remote_copy(
            src_ref=buffer.at[other],
            dst_ref=buffer.at[other],
            send_sem=send.at[step - 1],
            recv_sem=recv.at[other],
            device_id={"head": other},
            device_id_type=MESH,
        ).wait_recv()

    def state_copy(h):
        return pltpu.make_async_remote_copy(
            src_ref=state.at[h],
            dst_ref=state_in.at[h],
            send_sem=state_send.at[h],
            recv_sem=state_recv.at[h],
            device_id={"seq": lax.rem(z + 1, seqs)},
            device_id_type=MESH,
        )

    def later_copy(h):
        return pltpu.make_async_remote_copy(
            src_ref=later.at[h],
            dst_ref=later_in.at[h],
            send_sem=later_send.at[h],
            recv_sem=later_recv.at[h],
            device_id={"seq": lax.rem(z + seqs - 1, seqs)},
            device_id_type=MESH,
        )

    offsets = lax.broadcasted_iota(jnp.int32, (group, size), 0).astype(f32)

    def log_decay(h):
        return jnp.log1p(-jnp.full((1, size), decay_ref[h], f32))

    for load in loads[:5]:
        load.wait()
    places = z * group + lax.broadcasted_iota(jnp.int32, (group, npos), 0)
    chosen = places == positions_ref[...]
    select = jnp.where(chosen, 1.0, 0.0)
    turned = select.T
    select_rows[...] = turned.astype(bf16)
    stack[npos:, :] = jnp.zeros((stack.shape[0] - npos, stack.shape[1]), f32)
    picked = contract(select_rows[...], v_ref[0], 1, 0)
    stack[:npos, :] = picked
    stack[npos : npos + 4, :] = weight_ref[...]
    stack[npos + 4 : npos + 8, :] = rotation_ref[...]
    stack[npos + 8 : npos + 10, :] = refusal_ref[...]
    first[y] = jnp.zeros(first.shape[1:], f32)
    first[y, :, : stack.shape[0]] = contract(stack[npos:, :], stack[...], 1, 1, highest)
    pl.semaphore_wait(barrier, peers - 1 + members - 1)
    for step in range(1, peers):
        across(first, first_send, first_recv, step).start()

    for load in loads[5:8]:
        load.wait()

    def own_later(h):
        at = slice(h * size, (h + 1) * size)
        weighted = g_ref[0, :, at].astype(f32) * jnp.exp(offsets * log_decay(h))
        both = jnp.concatenate(split(weighted), axis=1)
        later[h] = halves(contract(q_ref[0, :, at], both, 0, 0))

    own_later(0)

    @pl.when(z == last)
    def _():
        later_copy(0).start()

    for h in range(1, heads):
        own_later(h)

    @pl.when(z == last)
    def _():
        for h in range(1, heads):
            later_copy(h).start()

    @pl.when(z == last)
    def _():
        later_in[...] = jnp.zeros_like(later_in)

    @pl.when(z == 0)
    def _():
        state_in[...] = jnp.zeros_like(state_in)

    between = lax.broadcasted_iota(jnp.int32, (group, group), 0) - lax.broadcasted_iota(
        jnp.int32, (group, group), 1
    )
    apart = jnp.maximum(between, 0).astype(f32)

    loads[8].wait()
    for step in range(1, peers):
        arrived(first, first_send, first_recv, step)
    summed = first[0]
    for peer in range(1, peers):
        summed = summed + first[peer]
    at_ref = npos + 8
    gram = [
        [summed[8 + a : 9 + a, at_ref + b : at_ref + b + 1] for b in range(2)] for a in range(2)
    ]
    determinant = gram[0][0] * gram[1][1] - gram[0][1] * gram[1][0]
    inverse = [
        [gram[1][1] / determinant, -gram[0][1] / determinant],
        [-gram[1][0] / determinant, gram[0][0] / determinant],
    ]
    coupling = [summed[4:8, at_ref + b : at_ref + b + 1] for b in range(2)]
    map_0 = coupling[0] * inverse[0][0] + coupling[1] * inverse[1][0]
    map_1 = coupling[0] * inverse[0][1] + coupling[1] * inverse[1][1]
    rotated = rotation_ref[...] - map_0 * refusal_ref[0:1, :] - map_1 * refusal_ref[1:2, :]
    rows[...] = jnp.zeros_like(rows)
    rows[0:4, :] = rotated
    rows[4:6, :] = refusal_ref[...]
    along = summed[8:10, :npos]
    rank = lax.broadcasted_iota(jnp.int32, (4, npos), 0)
    bias = jnp.zeros((4, npos), f32)
    for r in range(4):
        bias = jnp.where(rank == r, bias_ref[r], bias)
    code = (
        summed[0:4, :npos]
        + bias
        - (summed[4:8, :npos] - map_0 * along[0:1, :] - map_1 * along[1:2, :])
    )
    spread = contract(select, code, 1, 1, highest)
    loads[9].wait()

    def later_forward(h, carry):
        @pl.when(z < last)
        def _():
            later_copy(h).wait_recv()

        @pl.when(jnp.logical_and(z > 0, z < last))
        def _():
            later[h] = later[h] + jnp.exp(group * log_decay(h)) * later_in[h]
            later_copy(h).start()

        return carry

    def state_forward(h, carry):
        @pl.when(z > 0)
        def _():
            state_copy(h).wait_recv()

        @pl.when(jnp.logical_and(z > 0, z < last))
        def _():
            state[h] = state[h] + jnp.exp(group * log_decay(h)) * state_in[h]
            state_copy(h).start()

        return carry

    def own_state(h):
        at = slice(h * size, (h + 1) * size)
        value = v_ref[0, :, at].astype(f32)
        shift = spread[:, 0:1] * rows[0:1, at]
        for r in range(1, 4):
            shift = shift + spread[:, r : r + 1] * rows[r : r + 1, at]
        value = (value + shift).astype(bf16)
        moved[:, at] = value
        weighted = value.astype(f32) * jnp.exp((group - 1.0 - offsets) * log_decay(h))
        both = jnp.concatenate(split(weighted), axis=1)
        state[h] = halves(contract(k_ref[0, :, at], both, 0, 0))

    own_state(0)

    @pl.when(z == 0)
    def _():
        state_copy(0).start()

    for h in range(1, heads):
        own_state(h)

    @pl.when(z == 0)
    def _():
        for h in range(1, heads):
            state_copy(h).start()

    def local(h):
        at = slice(h * size, (h + 1) * size)
        table = jnp.where(between >= 0, jnp.exp(apart * log_decay(h)), 0.0)
        query, key = q_ref[0, :, at], k_ref[0, :, at]
        grad, value = g_ref[0, :, at], moved[:, at]
        mixing = (contract(query, key, 1, 1) * table).astype(bf16)
        mixed = (contract(grad, value, 1, 1) * table).astype(bf16)
        grad_moved[:, at] = contract(mixing, grad, 0, 0)
        inner_key[:, at] = contract(mixed, query, 0, 0)
        inner[:, at] = contract(mixing, value, 1, 0)
        inner_query[:, at] = contract(mixed, key, 1, 0)

    near = z == last - 1
    half = heads // 2
    one = jnp.where(near, min(1, heads), 0)
    two = jnp.where(near, min(2, heads), 0)
    ahead = jnp.where(near, min(4, heads), 0)
    state_ahead = jnp.where(jnp.logical_and(z == 1, z < last - 1), min(1, heads), 0)
    lax.fori_loop(0, one, later_forward, 0)
    for h in range(half):
        local(h)
    lax.fori_loop(one, two, later_forward, 0)
    lax.fori_loop(0, state_ahead, state_forward, 0)
    for h in range(half, heads):
        local(h)
    lax.fori_loop(two, ahead, later_forward, 0)

    def later_outer(h):
        at = pl.ds(pl.multiple_of(h * size, size), size)
        high, low = split(later_in[h])
        leave = jnp.exp((group - offsets) * log_decay(h))
        wide = grad_moved[:, at] + leave * halves(
            contract(k_ref[0, :, at], jnp.concatenate([high, low], axis=1), 1, 0)
        )
        grad_moved[:, at] = wide
        picks[:npos, at] = halves(
            contract(select_rows[...], jnp.concatenate(split(wide), axis=1), 1, 0)
        )
        grad_key = inner_key[:, at] + leave * halves(
            contract(moved[:, at], jnp.concatenate([high, low], axis=0), 1, 1)
        )
        grad_key_ref[0, :, at] = grad_key.astype(bf16)

    def state_outer(h):
        at = pl.ds(pl.multiple_of(h * size, size), size)
        high, low = split(state_in[h])
        enter = jnp.exp((offsets + 1.0) * log_decay(h))
        attended = inner[:, at] + enter * halves(
            contract(q_ref[0, :, at], jnp.concatenate([high, low], axis=1), 1, 0)
        )
        attended_ref[0, :, at] = attended.astype(bf16)
        grad_query = inner_query[:, at] + enter * halves(
            contract(g_ref[0, :, at], jnp.concatenate([high, low], axis=0), 1, 1)
        )
        grad_query_ref[0, :, at] = grad_query.astype(bf16)

    @pl.when(z == last)
    def _():
        for h in range(heads):
            later_outer(h)

    @pl.when(z < last)
    def _():
        def both_steps(i, carry):
            @pl.when(i + ahead < heads)
            def _():
                later_forward(jnp.minimum(i + ahead, heads - 1), 0)

            @pl.when(i + state_ahead < heads)
            def _():
                state_forward(jnp.minimum(i + state_ahead, heads - 1), 0)

            later_outer(i)
            state_outer(i)
            return carry

        lax.fori_loop(0, heads, both_steps, 0)

    stores[2].start()

    second[y] = jnp.zeros(second.shape[1:], f32)
    second[y, :, :npos] = contract(rows[...], picks[:npos, :], 1, 1, highest)
    for step in range(1, peers):
        across(second, second_send, second_recv, step).start()

    def part_copy(owner):
        target = owner * stride
        return pltpu.make_async_remote_copy(
            src_ref=pay.at[owner],
            dst_ref=parts.at[member],
            send_sem=parts_send.at[owner],
            recv_sem=parts_recv.at[member],
            device_id={"seq": target // docs, "dp": target % docs},
            device_id_type=MESH,
        )

    def finish_code():
        for step in range(1, peers):
            arrived(second, second_send, second_recv, step)
        sums = second[0]
        for peer in range(1, peers):
            sums = sums + second[peer]
        code_grad = sums[0:4, :npos]
        ahead = sums[4:6, :npos]
        projected = [
            jnp.sum(
                code * ahead[b : b + 1, :] - code_grad * along_own[b : b + 1, :],
                axis=1,
                keepdims=True,
            )
            for b in range(2)
        ]
        back_0 = projected[0] * inverse[0][0] + projected[1] * inverse[1][0]
        back_1 = projected[0] * inverse[0][1] + projected[1] * inverse[1][1]
        weight_part = contract(code_grad, stack[:npos, :], 1, 0, highest)
        rotation_part = (
            contract(code, picks[:npos, :], 1, 0, highest)
            - weight_part
            - back_0 * refusal_ref[0:1, :]
            - back_1 * refusal_ref[1:2, :]
        )
        bias_part = contract(jnp.ones((8, npos), f32), code_grad, 1, 1, highest)
        width = pay.shape[2]
        for owner in range(owners):
            at = slice(owner * width, (owner + 1) * width)
            pay[owner, 0:4, :] = rotation_part[:, at]
            pay[owner, 4:8, :] = weight_part[:, at]
            pay[owner, 8:16, :] = jnp.zeros((8, width), f32)
            pay[owner, 8:16, 0:4] = bias_part

            @pl.when(member == owner * stride)
            def _():
                parts[member] = pay[owner]

            @pl.when(member != owner * stride)
            def _():
                part_copy(owner).start()

        spread_grad = contract(select, code_grad, 1, 1, highest)
        for h in range(heads):
            at = slice(h * size, (h + 1) * size)
            wide = grad_moved[:, at]
            for r in range(4):
                wide = wide + spread_grad[:, r : r + 1] * (
                    weight_ref[r : r + 1, at] - rows[r : r + 1, at]
                )
            grad_value_ref[0, :, at] = wide.astype(bf16)
        stores[3].start()

    along_own = along

    @pl.when(z == last)
    def _():
        finish_code()

    @pl.when(z == last)
    def _():
        def rest(i, carry):
            state_forward(i, 0)
            state_outer(i)
            return carry

        lax.fori_loop(0, heads, rest, 0)

    stores[0].start()
    stores[1].start()

    @pl.when(z < last)
    def _():
        finish_code()

    mine = member // stride
    owning = lax.rem(member, stride) == 0

    def total_copy(step):
        other = lax.rem(member + step, members)
        return pltpu.make_async_remote_copy(
            src_ref=total.at[mine],
            dst_ref=total.at[mine],
            send_sem=total_send.at[step],
            recv_sem=total_recv.at[mine],
            device_id={"seq": other // docs, "dp": lax.rem(other, docs)},
            device_id_type=MESH,
        )

    def part_arrived(step, carry):
        other = lax.rem(member + step, members)
        pltpu.make_async_remote_copy(
            src_ref=pay.at[0],
            dst_ref=parts.at[other],
            send_sem=parts_send.at[0],
            recv_sem=parts_recv.at[other],
            device_id={"seq": other // docs, "dp": lax.rem(other, docs)},
            device_id_type=MESH,
        ).wait_recv()
        return carry

    def total_start(step, carry):
        total_copy(step).start()
        return carry

    def total_sent(step, carry):
        total_copy(step).wait_send()
        return carry

    @pl.when(owning)
    def _():
        lax.fori_loop(1, members, part_arrived, 0)
        total[mine] = jnp.sum(parts[...], axis=0)
        lax.fori_loop(1, members, total_start, 0)

    width = pay.shape[2]
    for owner in range(owners):

        @pl.when(member != owner * stride)
        def _():
            pltpu.make_async_remote_copy(
                src_ref=total.at[owner],
                dst_ref=total.at[owner],
                send_sem=total_send.at[0],
                recv_sem=total_recv.at[owner],
                device_id={"seq": (owner * stride) // docs, "dp": (owner * stride) % docs},
                device_id_type=MESH,
            ).wait_recv()

    for owner in range(owners):
        at = slice(owner * width, (owner + 1) * width)
        grad_rotation_ref[:, at] = total[owner, 0:4, :]
        grad_weight_ref[:, at] = total[owner, 4:8, :]
    grad_bias_ref[...] = total[0, 8:9, 0:4]
    for i in range(4, 7):
        stores[i].start()

    for i in range(7):
        stores[i].wait()
    for step in range(1, peers):
        across(first, first_send, first_recv, step).wait_send()
        across(second, second_send, second_recv, step).wait_send()

    def sent(h, carry):
        @pl.when(z < last)
        def _():
            state_copy(h).wait_send()

        @pl.when(z > 0)
        def _():
            later_copy(h).wait_send()

        return carry

    lax.fori_loop(0, heads, sent, 0)
    for owner in range(owners):

        @pl.when(member != owner * stride)
        def _():
            part_copy(owner).wait_send()

    @pl.when(owning)
    def _():
        lax.fori_loop(1, members, total_sent, 0)


def store(*refs):
    sources, targets, held, sems = refs[:7], refs[7:14], refs[14:21], refs[21]
    fetches = [pltpu.make_async_copy(sources[i], held[i], sems.at[0, i]) for i in range(7)]
    copies = [pltpu.make_async_copy(held[i], targets[i], sems.at[1, i]) for i in range(7)]
    for fetch in fetches:
        fetch.start()
    for fetch, copy in zip(fetches, copies):
        fetch.wait()
        copy.start()
    for copy in copies:
        copy.wait()


def shards(mesh, *arrays):
    (queries, key_rows, values, out_grad, decay_rate, rotation, refusal, weight, bias, positions) = (
        arrays
    )
    seqs, peers, docs = mesh.shape["seq"], mesh.shape["head"], mesh.shape["dp"]
    heads = decay_rate.shape[0]
    group, width = queries.shape[1], queries.shape[2]
    size = width // heads
    npos = positions.shape[1]
    members = seqs * docs
    owners = min(members, width // 128)
    limit = 60 * 1024 * 1024
    hbm = pl.BlockSpec(memory_space=pltpu.HBM)
    dma = pltpu.SemaphoreType.DMA
    square = (heads, size, size)
    big = jax.ShapeDtypeStruct(queries.shape, bf16)
    results = pl.pallas_call(
        functools.partial(kernel, (seqs, peers, docs, heads, owners)),
        out_shape=(
            big,
            big,
            big,
            big,
            jax.ShapeDtypeStruct(rotation.shape, f32),
            jax.ShapeDtypeStruct(weight.shape, f32),
            jax.ShapeDtypeStruct((1,) + bias.shape, f32),
        ),
        in_specs=[hbm] * 10,
        out_specs=(hbm,) * 7,
        scratch_shapes=[
            pltpu.VMEM(queries.shape, bf16),
            pltpu.VMEM(queries.shape, bf16),
            pltpu.VMEM(queries.shape, bf16),
            pltpu.VMEM(queries.shape, bf16),
            pltpu.VMEM(rotation.shape, f32),
            pltpu.VMEM(weight.shape, f32),
            pltpu.VMEM((1,) + bias.shape, f32),
            dma((7,)),
            pltpu.VMEM(queries.shape, bf16),
            pltpu.VMEM(queries.shape, bf16),
            pltpu.VMEM(queries.shape, bf16),
            pltpu.VMEM(queries.shape, bf16),
            pltpu.SMEM(decay_rate.shape, f32),
            pltpu.VMEM(rotation.shape, f32),
            pltpu.VMEM((2, width), f32),
            pltpu.VMEM(weight.shape, f32),
            pltpu.SMEM(bias.shape, f32),
            pltpu.VMEM(positions.shape, jnp.int32),
            dma((10,)),
            pltpu.VMEM((npos, group), bf16),
            pltpu.VMEM((group, width), f32),
            pltpu.VMEM((group, width), f32),
            pltpu.VMEM((group, width), f32),
            pltpu.VMEM((npos + 16, width), f32),
            pltpu.VMEM((npos, width), f32),
            pltpu.VMEM((8, width), f32),
            pltpu.VMEM((group, width), bf16),
            pltpu.VMEM((group, width), f32),
            pltpu.VMEM(square, f32),
            pltpu.VMEM(square, f32),
            pltpu.VMEM(square, f32),
            pltpu.VMEM(square, f32),
            pltpu.VMEM((peers, 16, 128), f32),
            pltpu.VMEM((peers, 8, 128), f32),
            pltpu.VMEM((owners, 16, width // owners), f32),
            pltpu.VMEM((members, 16, width // owners), f32),
            pltpu.VMEM((owners, 16, width // owners), f32),
            dma((peers,)),
            dma((peers,)),
            dma((peers,)),
            dma((peers,)),
            dma((heads,)),
            dma((heads,)),
            dma((heads,)),
            dma((heads,)),
            dma((owners,)),
            dma((members,)),
            dma((members,)),
            dma((owners,)),
        ],
        compiler_params=pltpu.CompilerParams(
            collective_id=0, has_side_effects=True, vmem_limit_bytes=limit
        ),
    )(queries, key_rows, values, out_grad, decay_rate, rotation, refusal.T, weight, bias, positions)
    results = pl.pallas_call(
        store,
        out_shape=tuple(jax.ShapeDtypeStruct(x.shape, x.dtype) for x in results),
        in_specs=[hbm] * 7,
        out_specs=(hbm,) * 7,
        scratch_shapes=[pltpu.VMEM(x.shape, x.dtype) for x in results] + [dma((2, 7))],
        compiler_params=pltpu.CompilerParams(vmem_limit_bytes=limit),
    )(*results)
    return results[:6] + (results[6].reshape(bias.shape),)


def solution(mesh):
    return jax.shard_map(
        functools.partial(shards, mesh),
        mesh=mesh,
        in_specs=(
            P("dp", "seq", "head"),
            P("dp", "seq", "head"),
            P("dp", "seq", "head"),
            P("dp", "seq", "head"),
            P("head"),
            P(None, "head"),
            P("head", None),
            P(None, "head"),
            P(),
            P("dp", None),
        ),
        out_specs=(
            P("dp", "seq", "head"),
            P("dp", "seq", "head"),
            P("dp", "seq", "head"),
            P("dp", "seq", "head"),
            P(None, "head"),
            P(None, "head"),
            P(),
        ),
        check_vma=False,
    )
```

```python
import functools
import jax
import jax.numpy as jnp
from jax import lax
from jax.experimental import pallas as pl
from jax.experimental.pallas import tpu as pltpu
from jax.sharding import PartitionSpec as P

highest = lax.Precision.HIGHEST
MESH = pl.DeviceIdType.MESH
f32 = jnp.float32
bf16 = jnp.bfloat16


def contract(a, b, da, db, precision=None):
    return lax.dot_general(
        a, b, (((da,), (db,)), ((), ())), precision=precision, preferred_element_type=f32
    )


def split(x):
    high = x.astype(bf16)
    return high, (x - high.astype(f32)).astype(bf16)


def halves(x):
    n = x.shape[1] // 2
    return x[:, :n] + x[:, n:]


def kernel(
    sizes,
    q_in,
    k_in,
    v_in,
    g_in,
    decay_in,
    rotation_in,
    refusal_in,
    weight_in,
    bias_in,
    positions_in,
    attended_out,
    grad_query_out,
    grad_key_out,
    grad_value_out,
    grad_rotation_out,
    grad_weight_out,
    grad_bias_out,
    attended_ref,
    grad_query_ref,
    grad_key_ref,
    grad_value_ref,
    grad_rotation_ref,
    grad_weight_ref,
    grad_bias_ref,
    store_sem,
    q_ref,
    k_ref,
    v_ref,
    g_ref,
    decay_ref,
    rotation_ref,
    refusal_ref,
    weight_ref,
    bias_ref,
    positions_ref,
    load_sem,
    select_rows,
    chosen_rows,
    inner,
    inner_query,
    inner_key,
    stack,
    picks,
    rows,
    moved,
    grad_moved,
    state,
    state_in,
    later,
    later_in,
    first,
    second,
    pay,
    parts,
    total,
    first_send,
    first_recv,
    second_send,
    second_recv,
    state_send,
    state_recv,
    later_send,
    later_recv,
    parts_send,
    parts_recv,
    total_send,
    total_recv,
):
    seqs, peers, docs, heads, owners = sizes
    group = q_ref.shape[1]
    size = q_ref.shape[2] // heads
    npos = positions_ref.shape[1]
    members = seqs * docs
    stride = members // owners
    z, y, c = lax.axis_index("seq"), lax.axis_index("head"), lax.axis_index("dp")
    last = seqs - 1
    member = z * docs + c

    loads = [
        pltpu.make_async_copy(source, target, load_sem.at[i])
        for i, (source, target) in enumerate(
            (
                (v_in, v_ref),
                (positions_in, positions_ref),
                (weight_in, weight_ref),
                (rotation_in, rotation_ref),
                (refusal_in, refusal_ref),
                (q_in, q_ref),
                (g_in, g_ref),
                (decay_in, decay_ref),
                (bias_in, bias_ref),
                (k_in, k_ref),
            )
        )
    ]
    for load in loads:
        load.start()
    stores = [
        pltpu.make_async_copy(source, target, store_sem.at[i])
        for i, (source, target) in enumerate(
            (
                (attended_ref, attended_out),
                (grad_query_ref, grad_query_out),
                (grad_key_ref, grad_key_out),
                (grad_value_ref, grad_value_out),
                (grad_rotation_ref, grad_rotation_out),
                (grad_weight_ref, grad_weight_out),
                (grad_bias_ref, grad_bias_out),
            )
        )
    ]
    barrier = pltpu.get_barrier_semaphore()
    for step in range(1, peers):
        pl.semaphore_signal(
            barrier, inc=1, device_id={"head": lax.rem(y + step, peers)}, device_id_type=MESH
        )

    def greet(step, carry):
        other = lax.rem(member + step, members)
        pl.semaphore_signal(
            barrier,
            inc=1,
            device_id={"seq": other // docs, "dp": lax.rem(other, docs)},
            device_id_type=MESH,
        )
        return carry

    lax.fori_loop(1, members, greet, 0)

    def across(buffer, send, recv, step):
        other = lax.rem(y + step, peers)
        return pltpu.make_async_remote_copy(
            src_ref=buffer.at[y],
            dst_ref=buffer.at[y],
            send_sem=send.at[step - 1],
            recv_sem=recv.at[y],
            device_id={"head": other},
            device_id_type=MESH,
        )

    def arrived(buffer, send, recv, step):
        other = lax.rem(y + step, peers)
        pltpu.make_async_remote_copy(
            src_ref=buffer.at[other],
            dst_ref=buffer.at[other],
            send_sem=send.at[step - 1],
            recv_sem=recv.at[other],
            device_id={"head": other},
            device_id_type=MESH,
        ).wait_recv()

    def state_copy(h):
        return pltpu.make_async_remote_copy(
            src_ref=state.at[h],
            dst_ref=state_in.at[h],
            send_sem=state_send.at[h],
            recv_sem=state_recv.at[h],
            device_id={"seq": lax.rem(z + 1, seqs)},
            device_id_type=MESH,
        )

    def later_copy(h):
        return pltpu.make_async_remote_copy(
            src_ref=later.at[h],
            dst_ref=later_in.at[h],
            send_sem=later_send.at[h],
            recv_sem=later_recv.at[h],
            device_id={"seq": lax.rem(z + seqs - 1, seqs)},
            device_id_type=MESH,
        )

    offsets = lax.broadcasted_iota(jnp.int32, (group, size), 0).astype(f32)

    def log_decay(h):
        return jnp.log1p(-jnp.full((1, size), decay_ref[h], f32))

    def project(ready):
        for load in loads[:5]:
            load.wait()
        places = z * group + lax.broadcasted_iota(jnp.int32, (group, npos), 0)
        chosen = places == positions_ref[...]
        chosen_rows[...] = jnp.where(chosen, 1.0, 0.0)
        turned = chosen_rows[...].T
        select_rows[...] = turned.astype(bf16)
        stack[npos:, :] = jnp.zeros((stack.shape[0] - npos, stack.shape[1]), f32)
        picked = contract(select_rows[...], v_ref[0], 1, 0)
        stack[:npos, :] = picked
        stack[npos : npos + 4, :] = weight_ref[...]
        stack[npos + 4 : npos + 8, :] = rotation_ref[...]
        stack[npos + 8 : npos + 10, :] = refusal_ref[...]
        first[y] = jnp.zeros(first.shape[1:], f32)
        first[y, :, : stack.shape[0]] = contract(stack[npos:, :], stack[...], 1, 1, highest)
        if not ready:
            pl.semaphore_wait(barrier, peers - 1 + members - 1)
        for step in range(1, peers):
            across(first, first_send, first_recv, step).start()

    def own_later(h):
        at = slice(h * size, (h + 1) * size)
        weighted = g_ref[0, :, at].astype(f32) * jnp.exp(offsets * log_decay(h))
        both = jnp.concatenate(split(weighted), axis=1)
        later[h] = halves(contract(q_ref[0, :, at], both, 0, 0))

    def own_laters():
        for load in loads[5:8]:
            load.wait()
        own_later(0)
        for h in range(1, heads):
            own_later(h)

    @pl.when(z == last)
    def _():
        for load in loads[5:8]:
            load.wait()
        own_later(0)
        pl.semaphore_wait(barrier, peers - 1 + members - 1)
        later_copy(0).start()
        for h in range(1, heads):
            own_later(h)
        for h in range(1, heads):
            later_copy(h).start()
        project(True)

    @pl.when(z < last)
    def _():
        project(False)
        own_laters()

    @pl.when(z == last)
    def _():
        later_in[...] = jnp.zeros_like(later_in)

    @pl.when(z == 0)
    def _():
        state_in[...] = jnp.zeros_like(state_in)

    between = lax.broadcasted_iota(jnp.int32, (group, group), 0) - lax.broadcasted_iota(
        jnp.int32, (group, group), 1
    )
    apart = jnp.maximum(between, 0).astype(f32)

    loads[8].wait()
    for step in range(1, peers):
        arrived(first, first_send, first_recv, step)
    summed = first[0]
    for peer in range(1, peers):
        summed = summed + first[peer]
    at_ref = npos + 8
    gram = [
        [summed[8 + a : 9 + a, at_ref + b : at_ref + b + 1] for b in range(2)] for a in range(2)
    ]
    determinant = gram[0][0] * gram[1][1] - gram[0][1] * gram[1][0]
    inverse = [
        [gram[1][1] / determinant, -gram[0][1] / determinant],
        [-gram[1][0] / determinant, gram[0][0] / determinant],
    ]
    coupling = [summed[4:8, at_ref + b : at_ref + b + 1] for b in range(2)]
    map_0 = coupling[0] * inverse[0][0] + coupling[1] * inverse[1][0]
    map_1 = coupling[0] * inverse[0][1] + coupling[1] * inverse[1][1]
    rotated = rotation_ref[...] - map_0 * refusal_ref[0:1, :] - map_1 * refusal_ref[1:2, :]
    rows[...] = jnp.zeros_like(rows)
    rows[0:4, :] = rotated
    rows[4:6, :] = refusal_ref[...]
    along = summed[8:10, :npos]
    rank = lax.broadcasted_iota(jnp.int32, (4, npos), 0)
    bias = jnp.zeros((4, npos), f32)
    for r in range(4):
        bias = jnp.where(rank == r, bias_ref[r], bias)
    code = (
        summed[0:4, :npos]
        + bias
        - (summed[4:8, :npos] - map_0 * along[0:1, :] - map_1 * along[1:2, :])
    )
    spread = contract(chosen_rows[...], code, 1, 1, highest)
    loads[9].wait()

    def later_forward(h, carry):
        @pl.when(z < last)
        def _():
            later_copy(h).wait_recv()

        @pl.when(jnp.logical_and(z > 0, z < last))
        def _():
            later[h] = later[h] + jnp.exp(group * log_decay(h)) * later_in[h]
            later_copy(h).start()

        return carry

    def state_forward(h, carry):
        @pl.when(z > 0)
        def _():
            state_copy(h).wait_recv()

        @pl.when(jnp.logical_and(z > 0, z < last))
        def _():
            state[h] = state[h] + jnp.exp(group * log_decay(h)) * state_in[h]
            state_copy(h).start()

        return carry

    def own_state(h):
        at = slice(h * size, (h + 1) * size)
        value = v_ref[0, :, at].astype(f32)
        shift = spread[:, 0:1] * rows[0:1, at]
        for r in range(1, 4):
            shift = shift + spread[:, r : r + 1] * rows[r : r + 1, at]
        value = (value + shift).astype(bf16)
        moved[:, at] = value
        weighted = value.astype(f32) * jnp.exp((group - 1.0 - offsets) * log_decay(h))
        both = jnp.concatenate(split(weighted), axis=1)
        state[h] = halves(contract(k_ref[0, :, at], both, 0, 0))

    own_state(0)

    @pl.when(z == 0)
    def _():
        state_copy(0).start()

    near = z == last - 1
    mid = jnp.logical_and(z == last - 2, z > 0)
    one = jnp.where(near, min(1, heads), 0)
    lax.fori_loop(0, one, later_forward, 0)
    for h in range(1, heads):
        own_state(h)

    @pl.when(z == 0)
    def _():
        for h in range(1, heads):
            state_copy(h).start()

    def local(h):
        at = slice(h * size, (h + 1) * size)
        table = jnp.where(between >= 0, jnp.exp(apart * log_decay(h)), 0.0)
        query, key = q_ref[0, :, at], k_ref[0, :, at]
        grad, value = g_ref[0, :, at], moved[:, at]
        mixing = (contract(query, key, 1, 1) * table).astype(bf16)
        mixed = (contract(grad, value, 1, 1) * table).astype(bf16)
        grad_moved[:, at] = contract(mixing, grad, 0, 0)
        inner_key[:, at] = contract(mixed, query, 0, 0)
        inner[:, at] = contract(mixing, value, 1, 0)
        inner_query[:, at] = contract(mixed, key, 1, 0)

    half = heads // 2
    two = jnp.where(near, min(2, heads), 0)
    three = jnp.where(near, min(3, heads), jnp.where(mid, min(1, heads), 0))
    ahead = jnp.where(near, min(4, heads), jnp.where(mid, min(1, heads), 0))
    state_ahead = jnp.where(jnp.logical_and(z == 1, z < last - 1), min(1, heads), 0)
    lax.fori_loop(one, two, later_forward, 0)
    for h in range(half):
        local(h)
    lax.fori_loop(two, three, later_forward, 0)
    lax.fori_loop(0, state_ahead, state_forward, 0)
    for h in range(half, heads):
        local(h)
    lax.fori_loop(three, ahead, later_forward, 0)

    def later_outer(h):
        at = pl.ds(pl.multiple_of(h * size, size), size)
        high, low = split(later_in[h])
        leave = jnp.exp((group - offsets) * log_decay(h))
        wide = grad_moved[:, at] + leave * halves(
            contract(k_ref[0, :, at], jnp.concatenate([high, low], axis=1), 1, 0)
        )
        grad_moved[:, at] = wide
        picks[:npos, at] = halves(
            contract(select_rows[...], jnp.concatenate(split(wide), axis=1), 1, 0)
        )
        grad_key = inner_key[:, at] + leave * halves(
            contract(moved[:, at], jnp.concatenate([high, low], axis=0), 1, 1)
        )
        grad_key_ref[0, :, at] = grad_key.astype(bf16)

    def state_outer(h):
        at = pl.ds(pl.multiple_of(h * size, size), size)
        high, low = split(state_in[h])
        enter = jnp.exp((offsets + 1.0) * log_decay(h))
        attended = inner[:, at] + enter * halves(
            contract(q_ref[0, :, at], jnp.concatenate([high, low], axis=1), 1, 0)
        )
        attended_ref[0, :, at] = attended.astype(bf16)
        grad_query = inner_query[:, at] + enter * halves(
            contract(g_ref[0, :, at], jnp.concatenate([high, low], axis=0), 1, 1)
        )
        grad_query_ref[0, :, at] = grad_query.astype(bf16)

    @pl.when(z == last)
    def _():
        for h in range(heads):
            later_outer(h)

    @pl.when(z < last)
    def _():
        def both_steps(i, carry):
            @pl.when(i + ahead < heads)
            def _():
                later_forward(jnp.minimum(i + ahead, heads - 1), 0)

            @pl.when(i + state_ahead < heads)
            def _():
                state_forward(jnp.minimum(i + state_ahead, heads - 1), 0)

            later_outer(i)
            state_outer(i)
            return carry

        lax.fori_loop(0, heads, both_steps, 0)

    stores[2].start()

    second[y] = jnp.zeros(second.shape[1:], f32)
    second[y, :, :npos] = contract(rows[...], picks[:npos, :], 1, 1, highest)
    for step in range(1, peers):
        across(second, second_send, second_recv, step).start()

    def part_copy(owner):
        target = owner * stride
        return pltpu.make_async_remote_copy(
            src_ref=pay.at[owner],
            dst_ref=parts.at[member],
            send_sem=parts_send.at[owner],
            recv_sem=parts_recv.at[member],
            device_id={"seq": target // docs, "dp": target % docs},
            device_id_type=MESH,
        )

    def finish_code():
        forth = contract(code, picks[:npos, :], 1, 0, highest)
        for step in range(1, peers):
            arrived(second, second_send, second_recv, step)
        sums = second[0]
        for peer in range(1, peers):
            sums = sums + second[peer]
        code_grad = sums[0:4, :npos]
        ahead = sums[4:6, :npos]
        projected = [
            jnp.sum(
                code * ahead[b : b + 1, :] - code_grad * along_own[b : b + 1, :],
                axis=1,
                keepdims=True,
            )
            for b in range(2)
        ]
        back_0 = projected[0] * inverse[0][0] + projected[1] * inverse[1][0]
        back_1 = projected[0] * inverse[0][1] + projected[1] * inverse[1][1]
        weight_part = contract(code_grad, stack[:npos, :], 1, 0, highest)
        rotation_part = (
            forth
            - weight_part
            - back_0 * refusal_ref[0:1, :]
            - back_1 * refusal_ref[1:2, :]
        )
        bias_part = contract(jnp.ones((8, npos), f32), code_grad, 1, 1, highest)
        width = pay.shape[2]
        for owner in range(owners):
            at = slice(owner * width, (owner + 1) * width)
            pay[owner, 0:4, :] = rotation_part[:, at]
            pay[owner, 4:8, :] = weight_part[:, at]
            pay[owner, 8:16, :] = jnp.zeros((8, width), f32)
            pay[owner, 8:16, 0:4] = bias_part

            @pl.when(member == owner * stride)
            def _():
                parts[member] = pay[owner]

            @pl.when(member != owner * stride)
            def _():
                part_copy(owner).start()

        spread_grad = contract(chosen_rows[...], code_grad, 1, 1, highest)
        for h in range(heads):
            at = slice(h * size, (h + 1) * size)
            wide = grad_moved[:, at]
            for r in range(4):
                wide = wide + spread_grad[:, r : r + 1] * (
                    weight_ref[r : r + 1, at] - rows[r : r + 1, at]
                )
            grad_value_ref[0, :, at] = wide.astype(bf16)
        stores[3].start()

    along_own = along

    @pl.when(z == last)
    def _():
        finish_code()

    @pl.when(z == last)
    def _():
        def rest(i, carry):
            state_forward(i, 0)
            state_outer(i)
            return carry

        lax.fori_loop(0, heads, rest, 0)

    stores[0].start()
    stores[1].start()

    @pl.when(z < last)
    def _():
        finish_code()

    mine = member // stride
    owning = lax.rem(member, stride) == 0

    def total_copy(step):
        other = lax.rem(member + step, members)
        return pltpu.make_async_remote_copy(
            src_ref=total.at[mine],
            dst_ref=total.at[mine],
            send_sem=total_send.at[step],
            recv_sem=total_recv.at[mine],
            device_id={"seq": other // docs, "dp": lax.rem(other, docs)},
            device_id_type=MESH,
        )

    def part_arrived(step, carry):
        other = lax.rem(member + step, members)
        pltpu.make_async_remote_copy(
            src_ref=pay.at[0],
            dst_ref=parts.at[other],
            send_sem=parts_send.at[0],
            recv_sem=parts_recv.at[other],
            device_id={"seq": other // docs, "dp": lax.rem(other, docs)},
            device_id_type=MESH,
        ).wait_recv()
        return carry

    def total_start(step, carry):
        total_copy(step).start()
        return carry

    def total_sent(step, carry):
        total_copy(step).wait_send()
        return carry

    @pl.when(owning)
    def _():
        lax.fori_loop(1, members, part_arrived, 0)
        total[mine] = jnp.sum(parts[...], axis=0)
        lax.fori_loop(1, members, total_start, 0)

    width = pay.shape[2]
    for owner in range(owners):

        @pl.when(member != owner * stride)
        def _():
            pltpu.make_async_remote_copy(
                src_ref=total.at[owner],
                dst_ref=total.at[owner],
                send_sem=total_send.at[0],
                recv_sem=total_recv.at[owner],
                device_id={"seq": (owner * stride) // docs, "dp": (owner * stride) % docs},
                device_id_type=MESH,
            ).wait_recv()

    for owner in range(owners):
        at = slice(owner * width, (owner + 1) * width)
        grad_rotation_ref[:, at] = total[owner, 0:4, :]
        grad_weight_ref[:, at] = total[owner, 4:8, :]
    grad_bias_ref[...] = total[0, 8:9, 0:4]
    for i in range(4, 7):
        stores[i].start()

    for i in range(7):
        stores[i].wait()
    for step in range(1, peers):
        across(first, first_send, first_recv, step).wait_send()
        across(second, second_send, second_recv, step).wait_send()

    def sent(h, carry):
        @pl.when(z < last)
        def _():
            state_copy(h).wait_send()

        @pl.when(z > 0)
        def _():
            later_copy(h).wait_send()

        return carry

    lax.fori_loop(0, heads, sent, 0)
    for owner in range(owners):

        @pl.when(member != owner * stride)
        def _():
            part_copy(owner).wait_send()

    @pl.when(owning)
    def _():
        lax.fori_loop(1, members, total_sent, 0)


def store(*refs):
    sources, targets, held, sems = refs[:7], refs[7:14], refs[14:21], refs[21]
    fetches = [pltpu.make_async_copy(sources[i], held[i], sems.at[0, i]) for i in range(7)]
    copies = [pltpu.make_async_copy(held[i], targets[i], sems.at[1, i]) for i in range(7)]
    for fetch in fetches:
        fetch.start()
    for fetch, copy in zip(fetches, copies):
        fetch.wait()
        copy.start()
    for copy in copies:
        copy.wait()


def shards(mesh, *arrays):
    (queries, key_rows, values, out_grad, decay_rate, rotation, refusal, weight, bias, positions) = (
        arrays
    )
    seqs, peers, docs = mesh.shape["seq"], mesh.shape["head"], mesh.shape["dp"]
    heads = decay_rate.shape[0]
    group, width = queries.shape[1], queries.shape[2]
    size = width // heads
    npos = positions.shape[1]
    members = seqs * docs
    owners = min(members, width // 128)
    limit = 60 * 1024 * 1024
    hbm = pl.BlockSpec(memory_space=pltpu.HBM)
    dma = pltpu.SemaphoreType.DMA
    square = (heads, size, size)
    big = jax.ShapeDtypeStruct(queries.shape, bf16)
    results = pl.pallas_call(
        functools.partial(kernel, (seqs, peers, docs, heads, owners)),
        out_shape=(
            big,
            big,
            big,
            big,
            jax.ShapeDtypeStruct(rotation.shape, f32),
            jax.ShapeDtypeStruct(weight.shape, f32),
            jax.ShapeDtypeStruct((1,) + bias.shape, f32),
        ),
        in_specs=[hbm] * 10,
        out_specs=(hbm,) * 7,
        scratch_shapes=[
            pltpu.VMEM(queries.shape, bf16),
            pltpu.VMEM(queries.shape, bf16),
            pltpu.VMEM(queries.shape, bf16),
            pltpu.VMEM(queries.shape, bf16),
            pltpu.VMEM(rotation.shape, f32),
            pltpu.VMEM(weight.shape, f32),
            pltpu.VMEM((1,) + bias.shape, f32),
            dma((7,)),
            pltpu.VMEM(queries.shape, bf16),
            pltpu.VMEM(queries.shape, bf16),
            pltpu.VMEM(queries.shape, bf16),
            pltpu.VMEM(queries.shape, bf16),
            pltpu.SMEM(decay_rate.shape, f32),
            pltpu.VMEM(rotation.shape, f32),
            pltpu.VMEM((2, width), f32),
            pltpu.VMEM(weight.shape, f32),
            pltpu.SMEM(bias.shape, f32),
            pltpu.VMEM(positions.shape, jnp.int32),
            dma((10,)),
            pltpu.VMEM((npos, group), bf16),
            pltpu.VMEM((group, npos), f32),
            pltpu.VMEM((group, width), f32),
            pltpu.VMEM((group, width), f32),
            pltpu.VMEM((group, width), f32),
            pltpu.VMEM((npos + 16, width), f32),
            pltpu.VMEM((npos, width), f32),
            pltpu.VMEM((8, width), f32),
            pltpu.VMEM((group, width), bf16),
            pltpu.VMEM((group, width), f32),
            pltpu.VMEM(square, f32),
            pltpu.VMEM(square, f32),
            pltpu.VMEM(square, f32),
            pltpu.VMEM(square, f32),
            pltpu.VMEM((peers, 16, 128), f32),
            pltpu.VMEM((peers, 8, 128), f32),
            pltpu.VMEM((owners, 16, width // owners), f32),
            pltpu.VMEM((members, 16, width // owners), f32),
            pltpu.VMEM((owners, 16, width // owners), f32),
            dma((peers,)),
            dma((peers,)),
            dma((peers,)),
            dma((peers,)),
            dma((heads,)),
            dma((heads,)),
            dma((heads,)),
            dma((heads,)),
            dma((owners,)),
            dma((members,)),
            dma((members,)),
            dma((owners,)),
        ],
        compiler_params=pltpu.CompilerParams(
            collective_id=0, has_side_effects=True, vmem_limit_bytes=limit
        ),
    )(queries, key_rows, values, out_grad, decay_rate, rotation, refusal.T, weight, bias, positions)
    results = pl.pallas_call(
        store,
        out_shape=tuple(jax.ShapeDtypeStruct(x.shape, x.dtype) for x in results),
        in_specs=[hbm] * 7,
        out_specs=(hbm,) * 7,
        scratch_shapes=[pltpu.VMEM(x.shape, x.dtype) for x in results] + [dma((2, 7))],
        compiler_params=pltpu.CompilerParams(vmem_limit_bytes=limit),
    )(*results)
    return results[:6] + (results[6].reshape(bias.shape),)


def solution(mesh):
    return jax.shard_map(
        functools.partial(shards, mesh),
        mesh=mesh,
        in_specs=(
            P("dp", "seq", "head"),
            P("dp", "seq", "head"),
            P("dp", "seq", "head"),
            P("dp", "seq", "head"),
            P("head"),
            P(None, "head"),
            P("head", None),
            P(None, "head"),
            P(),
            P("dp", None),
        ),
        out_specs=(
            P("dp", "seq", "head"),
            P("dp", "seq", "head"),
            P("dp", "seq", "head"),
            P("dp", "seq", "head"),
            P(None, "head"),
            P(None, "head"),
            P(),
        ),
        check_vma=False,
    )
```

```python
import functools
import jax
import jax.numpy as jnp
from jax import lax
from jax.experimental import pallas as pl
from jax.experimental.pallas import tpu as pltpu
from jax.sharding import PartitionSpec as P

highest = lax.Precision.HIGHEST
MESH = pl.DeviceIdType.MESH
f32 = jnp.float32
bf16 = jnp.bfloat16


def contract(a, b, da, db, precision=None):
    return lax.dot_general(
        a, b, (((da,), (db,)), ((), ())), precision=precision, preferred_element_type=f32
    )


def split(x):
    high = x.astype(bf16)
    return high, (x - high.astype(f32)).astype(bf16)


def halves(x):
    n = x.shape[1] // 2
    return x[:, :n] + x[:, n:]


def kernel(
    sizes,
    q_in,
    k_in,
    v_in,
    g_in,
    decay_in,
    rotation_in,
    refusal_in,
    weight_in,
    bias_in,
    positions_in,
    attended_out,
    grad_query_out,
    grad_key_out,
    grad_value_out,
    grad_rotation_out,
    grad_weight_out,
    grad_bias_out,
    attended_ref,
    grad_query_ref,
    grad_key_ref,
    grad_value_ref,
    grad_rotation_ref,
    grad_weight_ref,
    grad_bias_ref,
    store_sem,
    q_ref,
    k_ref,
    v_ref,
    g_ref,
    decay_ref,
    rotation_ref,
    refusal_ref,
    weight_ref,
    bias_ref,
    positions_ref,
    load_sem,
    select_rows,
    chosen_rows,
    inner,
    inner_query,
    inner_key,
    stack,
    picks,
    rows,
    moved,
    grad_moved,
    state,
    state_in,
    later,
    later_in,
    first,
    second,
    pay,
    parts,
    total,
    first_send,
    first_recv,
    second_send,
    second_recv,
    state_send,
    state_recv,
    later_send,
    later_recv,
    parts_send,
    parts_recv,
    total_send,
    total_recv,
):
    seqs, peers, docs, heads, owners = sizes
    group = q_ref.shape[1]
    size = q_ref.shape[2] // heads
    npos = positions_ref.shape[1]
    members = seqs * docs
    stride = members // owners
    z, y, c = lax.axis_index("seq"), lax.axis_index("head"), lax.axis_index("dp")
    last = seqs - 1
    member = z * docs + c

    loads = [
        pltpu.make_async_copy(source, target, load_sem.at[i])
        for i, (source, target) in enumerate(
            (
                (v_in, v_ref),
                (positions_in, positions_ref),
                (weight_in, weight_ref),
                (rotation_in, rotation_ref),
                (refusal_in, refusal_ref),
                (q_in, q_ref),
                (g_in, g_ref),
                (decay_in, decay_ref),
                (bias_in, bias_ref),
                (k_in, k_ref),
            )
        )
    ]
    for load in loads:
        load.start()
    stores = [
        pltpu.make_async_copy(source, target, store_sem.at[i])
        for i, (source, target) in enumerate(
            (
                (attended_ref, attended_out),
                (grad_query_ref, grad_query_out),
                (grad_key_ref, grad_key_out),
                (grad_value_ref, grad_value_out),
                (grad_rotation_ref, grad_rotation_out),
                (grad_weight_ref, grad_weight_out),
                (grad_bias_ref, grad_bias_out),
            )
        )
    ]
    barrier = pltpu.get_barrier_semaphore()
    for step in range(1, peers):
        pl.semaphore_signal(
            barrier, inc=1, device_id={"head": lax.rem(y + step, peers)}, device_id_type=MESH
        )

    def greet(step, carry):
        other = lax.rem(member + step, members)
        pl.semaphore_signal(
            barrier,
            inc=1,
            device_id={"seq": other // docs, "dp": lax.rem(other, docs)},
            device_id_type=MESH,
        )
        return carry

    lax.fori_loop(1, members, greet, 0)

    def across(buffer, send, recv, step):
        other = lax.rem(y + step, peers)
        return pltpu.make_async_remote_copy(
            src_ref=buffer.at[y],
            dst_ref=buffer.at[y],
            send_sem=send.at[step - 1],
            recv_sem=recv.at[y],
            device_id={"head": other},
            device_id_type=MESH,
        )

    def arrived(buffer, send, recv, step):
        other = lax.rem(y + step, peers)
        pltpu.make_async_remote_copy(
            src_ref=buffer.at[other],
            dst_ref=buffer.at[other],
            send_sem=send.at[step - 1],
            recv_sem=recv.at[other],
            device_id={"head": other},
            device_id_type=MESH,
        ).wait_recv()

    def state_copy(h):
        return pltpu.make_async_remote_copy(
            src_ref=state.at[h],
            dst_ref=state_in.at[h],
            send_sem=state_send.at[h],
            recv_sem=state_recv.at[h],
            device_id={"seq": lax.rem(z + 1, seqs)},
            device_id_type=MESH,
        )

    def later_copy(h):
        return pltpu.make_async_remote_copy(
            src_ref=later.at[h],
            dst_ref=later_in.at[h],
            send_sem=later_send.at[h],
            recv_sem=later_recv.at[h],
            device_id={"seq": lax.rem(z + seqs - 1, seqs)},
            device_id_type=MESH,
        )

    offsets = lax.broadcasted_iota(jnp.int32, (group, size), 0).astype(f32)

    def log_decay(h):
        return jnp.log1p(-jnp.full((1, size), decay_ref[h], f32))

    def project(ready):
        for load in loads[:5]:
            load.wait()
        places = z * group + lax.broadcasted_iota(jnp.int32, (group, npos), 0)
        chosen = places == positions_ref[...]
        chosen_rows[...] = jnp.where(chosen, 1.0, 0.0)
        turned = chosen_rows[...].T
        select_rows[...] = turned.astype(bf16)
        stack[npos:, :] = jnp.zeros((stack.shape[0] - npos, stack.shape[1]), f32)
        picked = contract(select_rows[...], v_ref[0], 1, 0)
        stack[:npos, :] = picked
        stack[npos : npos + 4, :] = weight_ref[...]
        stack[npos + 4 : npos + 8, :] = rotation_ref[...]
        stack[npos + 8 : npos + 10, :] = refusal_ref[...]
        first[y] = jnp.zeros(first.shape[1:], f32)
        first[y, :, : stack.shape[0]] = contract(stack[npos:, :], stack[...], 1, 1, highest)
        if not ready:
            pl.semaphore_wait(barrier, peers - 1 + members - 1)
        for step in range(1, peers):
            across(first, first_send, first_recv, step).start()

    def own_later(h):
        at = slice(h * size, (h + 1) * size)
        weighted = g_ref[0, :, at].astype(f32) * jnp.exp(offsets * log_decay(h))
        both = jnp.concatenate(split(weighted), axis=1)
        later[h] = halves(contract(q_ref[0, :, at], both, 0, 0))

    def own_laters():
        for load in loads[5:8]:
            load.wait()
        own_later(0)
        for h in range(1, heads):
            own_later(h)

    @pl.when(z == last)
    def _():
        for load in loads[5:8]:
            load.wait()
        own_later(0)
        pl.semaphore_wait(barrier, peers - 1 + members - 1)
        later_copy(0).start()
        for h in range(1, heads):
            own_later(h)
        for h in range(1, heads):
            later_copy(h).start()
        project(True)

    @pl.when(z < last)
    def _():
        project(False)
        own_laters()

    @pl.when(z == last)
    def _():
        later_in[...] = jnp.zeros_like(later_in)

    @pl.when(z == 0)
    def _():
        state_in[...] = jnp.zeros_like(state_in)

    between = lax.broadcasted_iota(jnp.int32, (group, group), 0) - lax.broadcasted_iota(
        jnp.int32, (group, group), 1
    )
    apart = jnp.maximum(between, 0).astype(f32)

    loads[8].wait()
    for step in range(1, peers):
        arrived(first, first_send, first_recv, step)
    summed = first[0]
    for peer in range(1, peers):
        summed = summed + first[peer]
    at_ref = npos + 8
    gram = [
        [summed[8 + a : 9 + a, at_ref + b : at_ref + b + 1] for b in range(2)] for a in range(2)
    ]
    determinant = gram[0][0] * gram[1][1] - gram[0][1] * gram[1][0]
    inverse = [
        [gram[1][1] / determinant, -gram[0][1] / determinant],
        [-gram[1][0] / determinant, gram[0][0] / determinant],
    ]
    coupling = [summed[4:8, at_ref + b : at_ref + b + 1] for b in range(2)]
    map_0 = coupling[0] * inverse[0][0] + coupling[1] * inverse[1][0]
    map_1 = coupling[0] * inverse[0][1] + coupling[1] * inverse[1][1]
    rotated = rotation_ref[...] - map_0 * refusal_ref[0:1, :] - map_1 * refusal_ref[1:2, :]
    rows[...] = jnp.zeros_like(rows)
    rows[0:4, :] = rotated
    rows[4:6, :] = refusal_ref[...]
    along = summed[8:10, :npos]
    rank = lax.broadcasted_iota(jnp.int32, (4, npos), 0)
    bias = jnp.zeros((4, npos), f32)
    for r in range(4):
        bias = jnp.where(rank == r, bias_ref[r], bias)
    code = (
        summed[0:4, :npos]
        + bias
        - (summed[4:8, :npos] - map_0 * along[0:1, :] - map_1 * along[1:2, :])
    )
    spread = contract(chosen_rows[...], code, 1, 1, highest)
    loads[9].wait()

    def later_forward(h, carry):
        @pl.when(z < last)
        def _():
            later_copy(h).wait_recv()

        @pl.when(jnp.logical_and(z > 0, z < last))
        def _():
            later[h] = later[h] + jnp.exp(group * log_decay(h)) * later_in[h]
            later_copy(h).start()

        return carry

    def state_forward(h, carry):
        @pl.when(z > 0)
        def _():
            state_copy(h).wait_recv()

        @pl.when(jnp.logical_and(z > 0, z < last))
        def _():
            state[h] = state[h] + jnp.exp(group * log_decay(h)) * state_in[h]
            state_copy(h).start()

        return carry

    def own_state(h):
        at = slice(h * size, (h + 1) * size)
        value = v_ref[0, :, at].astype(f32)
        shift = spread[:, 0:1] * rows[0:1, at]
        for r in range(1, 4):
            shift = shift + spread[:, r : r + 1] * rows[r : r + 1, at]
        value = (value + shift).astype(bf16)
        moved[:, at] = value
        weighted = value.astype(f32) * jnp.exp((group - 1.0 - offsets) * log_decay(h))
        both = jnp.concatenate(split(weighted), axis=1)
        state[h] = halves(contract(k_ref[0, :, at], both, 0, 0))

    own_state(0)

    @pl.when(z == 0)
    def _():
        state_copy(0).start()

    near = z == last - 1
    mid = jnp.logical_and(z == last - 2, z > 0)
    one = jnp.where(near, min(1, heads), 0)
    lax.fori_loop(0, one, later_forward, 0)
    for h in range(1, heads):
        own_state(h)

    @pl.when(z == 0)
    def _():
        for h in range(1, heads):
            state_copy(h).start()

    def local(h):
        at = slice(h * size, (h + 1) * size)
        table = jnp.where(between >= 0, jnp.exp(apart * log_decay(h)), 0.0)
        query, key = q_ref[0, :, at], k_ref[0, :, at]
        grad, value = g_ref[0, :, at], moved[:, at]
        mixing = (contract(query, key, 1, 1) * table).astype(bf16)
        mixed = (contract(grad, value, 1, 1) * table).astype(bf16)
        grad_moved[:, at] = contract(mixing, grad, 0, 0)
        inner_key[:, at] = contract(mixed, query, 0, 0)
        inner[:, at] = contract(mixing, value, 1, 0)
        inner_query[:, at] = contract(mixed, key, 1, 0)

    half = heads // 2
    two = jnp.where(near, min(2, heads), 0)
    three = jnp.where(near, min(3, heads), jnp.where(mid, min(1, heads), 0))
    ahead = jnp.where(near, min(5, heads), jnp.where(mid, min(1, heads), 0))
    far = jnp.logical_and(z == 1, z < last - 1)
    state_one = jnp.where(far, min(1, heads), 0)
    state_ahead = jnp.where(far, min(2, heads), 0)
    lax.fori_loop(one, two, later_forward, 0)
    for h in range(half):
        local(h)
    lax.fori_loop(two, three, later_forward, 0)
    lax.fori_loop(0, state_one, state_forward, 0)
    for h in range(half, heads):
        local(h)
    lax.fori_loop(three, ahead, later_forward, 0)
    lax.fori_loop(state_one, state_ahead, state_forward, 0)

    def later_outer(h):
        at = pl.ds(pl.multiple_of(h * size, size), size)
        high, low = split(later_in[h])
        leave = jnp.exp((group - offsets) * log_decay(h))
        wide = grad_moved[:, at] + leave * halves(
            contract(k_ref[0, :, at], jnp.concatenate([high, low], axis=1), 1, 0)
        )
        grad_moved[:, at] = wide
        picks[:npos, at] = halves(
            contract(select_rows[...], jnp.concatenate(split(wide), axis=1), 1, 0)
        )
        grad_key = inner_key[:, at] + leave * halves(
            contract(moved[:, at], jnp.concatenate([high, low], axis=0), 1, 1)
        )
        grad_key_ref[0, :, at] = grad_key.astype(bf16)

    def state_outer(h):
        at = pl.ds(pl.multiple_of(h * size, size), size)
        high, low = split(state_in[h])
        enter = jnp.exp((offsets + 1.0) * log_decay(h))
        attended = inner[:, at] + enter * halves(
            contract(q_ref[0, :, at], jnp.concatenate([high, low], axis=1), 1, 0)
        )
        attended_ref[0, :, at] = attended.astype(bf16)
        grad_query = inner_query[:, at] + enter * halves(
            contract(g_ref[0, :, at], jnp.concatenate([high, low], axis=0), 1, 1)
        )
        grad_query_ref[0, :, at] = grad_query.astype(bf16)

    @pl.when(z == last)
    def _():
        for h in range(heads):
            later_outer(h)

    @pl.when(z < last)
    def _():
        def both_steps(i, carry):
            @pl.when(i + ahead < heads)
            def _():
                later_forward(jnp.minimum(i + ahead, heads - 1), 0)

            @pl.when(i + state_ahead < heads)
            def _():
                state_forward(jnp.minimum(i + state_ahead, heads - 1), 0)

            later_outer(i)
            state_outer(i)
            return carry

        lax.fori_loop(0, heads, both_steps, 0)

    stores[2].start()

    second[y] = jnp.zeros(second.shape[1:], f32)
    second[y, :, :npos] = contract(rows[...], picks[:npos, :], 1, 1, highest)
    for step in range(1, peers):
        across(second, second_send, second_recv, step).start()

    def part_copy(owner):
        target = owner * stride
        return pltpu.make_async_remote_copy(
            src_ref=pay.at[owner],
            dst_ref=parts.at[member],
            send_sem=parts_send.at[owner],
            recv_sem=parts_recv.at[member],
            device_id={"seq": target // docs, "dp": target % docs},
            device_id_type=MESH,
        )

    def finish_code():
        forth = contract(code, picks[:npos, :], 1, 0, highest)
        for step in range(1, peers):
            arrived(second, second_send, second_recv, step)
        sums = second[0]
        for peer in range(1, peers):
            sums = sums + second[peer]
        code_grad = sums[0:4, :npos]
        ahead = sums[4:6, :npos]
        projected = [
            jnp.sum(
                code * ahead[b : b + 1, :] - code_grad * along_own[b : b + 1, :],
                axis=1,
                keepdims=True,
            )
            for b in range(2)
        ]
        back_0 = projected[0] * inverse[0][0] + projected[1] * inverse[1][0]
        back_1 = projected[0] * inverse[0][1] + projected[1] * inverse[1][1]
        weight_part = contract(code_grad, stack[:npos, :], 1, 0, highest)
        rotation_part = (
            forth
            - weight_part
            - back_0 * refusal_ref[0:1, :]
            - back_1 * refusal_ref[1:2, :]
        )
        bias_part = contract(jnp.ones((8, npos), f32), code_grad, 1, 1, highest)
        width = pay.shape[2]
        for owner in range(owners):
            at = slice(owner * width, (owner + 1) * width)
            pay[owner, 0:4, :] = rotation_part[:, at]
            pay[owner, 4:8, :] = weight_part[:, at]
            pay[owner, 8:16, :] = jnp.zeros((8, width), f32)
            pay[owner, 8:16, 0:4] = bias_part

            @pl.when(member == owner * stride)
            def _():
                parts[member] = pay[owner]

            @pl.when(member != owner * stride)
            def _():
                part_copy(owner).start()

        spread_grad = contract(chosen_rows[...], code_grad, 1, 1, highest)
        for h in range(heads):
            at = slice(h * size, (h + 1) * size)
            wide = grad_moved[:, at]
            for r in range(4):
                wide = wide + spread_grad[:, r : r + 1] * (
                    weight_ref[r : r + 1, at] - rows[r : r + 1, at]
                )
            grad_value_ref[0, :, at] = wide.astype(bf16)
        stores[3].start()

    along_own = along

    @pl.when(z == last)
    def _():
        finish_code()

    @pl.when(z == last)
    def _():
        def rest(i, carry):
            state_forward(i, 0)
            state_outer(i)
            return carry

        lax.fori_loop(0, heads, rest, 0)

    stores[0].start()
    stores[1].start()

    @pl.when(z < last)
    def _():
        finish_code()

    mine = member // stride
    owning = lax.rem(member, stride) == 0

    def total_copy(step):
        other = lax.rem(member + step, members)
        return pltpu.make_async_remote_copy(
            src_ref=total.at[mine],
            dst_ref=total.at[mine],
            send_sem=total_send.at[step],
            recv_sem=total_recv.at[mine],
            device_id={"seq": other // docs, "dp": lax.rem(other, docs)},
            device_id_type=MESH,
        )

    def part_arrived(step, carry):
        other = lax.rem(member + step, members)
        pltpu.make_async_remote_copy(
            src_ref=pay.at[0],
            dst_ref=parts.at[other],
            send_sem=parts_send.at[0],
            recv_sem=parts_recv.at[other],
            device_id={"seq": other // docs, "dp": lax.rem(other, docs)},
            device_id_type=MESH,
        ).wait_recv()
        return carry

    def total_start(step, carry):
        total_copy(step).start()
        return carry

    def total_sent(step, carry):
        total_copy(step).wait_send()
        return carry

    @pl.when(owning)
    def _():
        lax.fori_loop(1, members, part_arrived, 0)
        total[mine] = jnp.sum(parts[...], axis=0)
        lax.fori_loop(1, members, total_start, 0)

    width = pay.shape[2]
    for owner in range(owners):

        @pl.when(member != owner * stride)
        def _():
            pltpu.make_async_remote_copy(
                src_ref=total.at[owner],
                dst_ref=total.at[owner],
                send_sem=total_send.at[0],
                recv_sem=total_recv.at[owner],
                device_id={"seq": (owner * stride) // docs, "dp": (owner * stride) % docs},
                device_id_type=MESH,
            ).wait_recv()

    for owner in range(owners):
        at = slice(owner * width, (owner + 1) * width)
        grad_rotation_ref[:, at] = total[owner, 0:4, :]
        grad_weight_ref[:, at] = total[owner, 4:8, :]
    grad_bias_ref[...] = total[0, 8:9, 0:4]
    for i in range(4, 7):
        stores[i].start()

    for i in range(7):
        stores[i].wait()
    for step in range(1, peers):
        across(first, first_send, first_recv, step).wait_send()
        across(second, second_send, second_recv, step).wait_send()

    def sent(h, carry):
        @pl.when(z < last)
        def _():
            state_copy(h).wait_send()

        @pl.when(z > 0)
        def _():
            later_copy(h).wait_send()

        return carry

    lax.fori_loop(0, heads, sent, 0)
    for owner in range(owners):

        @pl.when(member != owner * stride)
        def _():
            part_copy(owner).wait_send()

    @pl.when(owning)
    def _():
        lax.fori_loop(1, members, total_sent, 0)


def store(*refs):
    sources, targets, held, sems = refs[:7], refs[7:14], refs[14:21], refs[21]
    fetches = [pltpu.make_async_copy(sources[i], held[i], sems.at[0, i]) for i in range(7)]
    copies = [pltpu.make_async_copy(held[i], targets[i], sems.at[1, i]) for i in range(7)]
    for fetch in fetches:
        fetch.start()
    for fetch, copy in zip(fetches, copies):
        fetch.wait()
        copy.start()
    for copy in copies:
        copy.wait()


def shards(mesh, *arrays):
    (queries, key_rows, values, out_grad, decay_rate, rotation, refusal, weight, bias, positions) = (
        arrays
    )
    seqs, peers, docs = mesh.shape["seq"], mesh.shape["head"], mesh.shape["dp"]
    heads = decay_rate.shape[0]
    group, width = queries.shape[1], queries.shape[2]
    size = width // heads
    npos = positions.shape[1]
    members = seqs * docs
    owners = min(members, width // 128)
    limit = 60 * 1024 * 1024
    hbm = pl.BlockSpec(memory_space=pltpu.HBM)
    dma = pltpu.SemaphoreType.DMA
    square = (heads, size, size)
    big = jax.ShapeDtypeStruct(queries.shape, bf16)
    results = pl.pallas_call(
        functools.partial(kernel, (seqs, peers, docs, heads, owners)),
        out_shape=(
            big,
            big,
            big,
            big,
            jax.ShapeDtypeStruct(rotation.shape, f32),
            jax.ShapeDtypeStruct(weight.shape, f32),
            jax.ShapeDtypeStruct((1,) + bias.shape, f32),
        ),
        in_specs=[hbm] * 10,
        out_specs=(hbm,) * 7,
        scratch_shapes=[
            pltpu.VMEM(queries.shape, bf16),
            pltpu.VMEM(queries.shape, bf16),
            pltpu.VMEM(queries.shape, bf16),
            pltpu.VMEM(queries.shape, bf16),
            pltpu.VMEM(rotation.shape, f32),
            pltpu.VMEM(weight.shape, f32),
            pltpu.VMEM((1,) + bias.shape, f32),
            dma((7,)),
            pltpu.VMEM(queries.shape, bf16),
            pltpu.VMEM(queries.shape, bf16),
            pltpu.VMEM(queries.shape, bf16),
            pltpu.VMEM(queries.shape, bf16),
            pltpu.SMEM(decay_rate.shape, f32),
            pltpu.VMEM(rotation.shape, f32),
            pltpu.VMEM((2, width), f32),
            pltpu.VMEM(weight.shape, f32),
            pltpu.SMEM(bias.shape, f32),
            pltpu.VMEM(positions.shape, jnp.int32),
            dma((10,)),
            pltpu.VMEM((npos, group), bf16),
            pltpu.VMEM((group, npos), f32),
            pltpu.VMEM((group, width), f32),
            pltpu.VMEM((group, width), f32),
            pltpu.VMEM((group, width), f32),
            pltpu.VMEM((npos + 16, width), f32),
            pltpu.VMEM((npos, width), f32),
            pltpu.VMEM((8, width), f32),
            pltpu.VMEM((group, width), bf16),
            pltpu.VMEM((group, width), f32),
            pltpu.VMEM(square, f32),
            pltpu.VMEM(square, f32),
            pltpu.VMEM(square, f32),
            pltpu.VMEM(square, f32),
            pltpu.VMEM((peers, 16, 128), f32),
            pltpu.VMEM((peers, 8, 128), f32),
            pltpu.VMEM((owners, 16, width // owners), f32),
            pltpu.VMEM((members, 16, width // owners), f32),
            pltpu.VMEM((owners, 16, width // owners), f32),
            dma((peers,)),
            dma((peers,)),
            dma((peers,)),
            dma((peers,)),
            dma((heads,)),
            dma((heads,)),
            dma((heads,)),
            dma((heads,)),
            dma((owners,)),
            dma((members,)),
            dma((members,)),
            dma((owners,)),
        ],
        compiler_params=pltpu.CompilerParams(
            collective_id=0, has_side_effects=True, vmem_limit_bytes=limit
        ),
    )(queries, key_rows, values, out_grad, decay_rate, rotation, refusal.T, weight, bias, positions)
    results = pl.pallas_call(
        store,
        out_shape=tuple(jax.ShapeDtypeStruct(x.shape, x.dtype) for x in results),
        in_specs=[hbm] * 7,
        out_specs=(hbm,) * 7,
        scratch_shapes=[pltpu.VMEM(x.shape, x.dtype) for x in results] + [dma((2, 7))],
        compiler_params=pltpu.CompilerParams(vmem_limit_bytes=limit),
    )(*results)
    return results[:6] + (results[6].reshape(bias.shape),)


def solution(mesh):
    return jax.shard_map(
        functools.partial(shards, mesh),
        mesh=mesh,
        in_specs=(
            P("dp", "seq", "head"),
            P("dp", "seq", "head"),
            P("dp", "seq", "head"),
            P("dp", "seq", "head"),
            P("head"),
            P(None, "head"),
            P("head", None),
            P(None, "head"),
            P(),
            P("dp", None),
        ),
        out_specs=(
            P("dp", "seq", "head"),
            P("dp", "seq", "head"),
            P("dp", "seq", "head"),
            P("dp", "seq", "head"),
            P(None, "head"),
            P(None, "head"),
            P(),
        ),
        check_vma=False,
    )
```
